32 devices in a mesh: video: 2 (over x), tm: 16 (over z, y, core).
Axes of the slice: x: 2, y: 2, z: 4, core: 2. Of those that a mesh axis runs over, the one named last changes fastest.
Arguments:
- video: bfloat16 [32, 3, 32, 960], P(('video', 'tm')), parts along dimension 0, may hold values from -6 to 6
- w_in: float32 [32, 3], replicated, may hold values from -3.5 to 3.5
- b_in: float32 [32], replicated, may hold values from -2 to 2
- w_out: float32 [3, 32], replicated, may hold values from -1 to 1
- b_out: float32 [3], replicated, may hold values from -2 to 2
- screen: float32 [3], replicated, may hold values from 0.5 to 2
Outputs:
- consistent: float32 [32, 3, 32, 960], P('video', None, 'tm'), parts along dimension 0
The draws below stay inside these ranges and needn't reach their ends.
There are 2 independent parts, one for each index of `video`. The reference program is written for one: setup_inputs(seed, part) draws one part's arguments, and reference() takes and returns one part's arrays. A program takes and returns all parts, laid end to end along the dimension named above; an argument that names none is the same for every part. Nothing has to cross between parts.
All inputs are finite; a program needn't handle non-finite values.
Results may differ from the reference program's by a relative error of at most 0.0036.
Values may be sent and summed in bfloat16 or wider, within the bound.
No kernel may reach another device: no remote copies, remote signals or barrier semaphores. Data moves between devices by JAX's collectives and lax.ppermute only.
A program may use at most 64 MiB of HBM per device.

```python
import math
import jax
import jax.numpy as jnp
from jax import lax

COLS = 960
UNITS = 32
ITERS = 3
FRAMES = 16
ROWS = 32


def draw_video(key, part):
    first_key = jax.random.fold_in(key, 0)
    shape = (FRAMES, 3, ROWS, COLS)
    ramp = 0.5 + jnp.arange(FRAMES, dtype=jnp.float32) / max(FRAMES - 1, 1)
    base = jnp.clip(jax.random.normal(first_key, shape, jnp.float32), -4.0, 4.0)
    return (base * ramp[:, None, None, None]).astype(jnp.bfloat16)


def noise(key, shape, width, reach, kind=jnp.bfloat16):
    values = width * jax.random.normal(key, shape, jnp.float32)
    return jnp.clip(values, min=-reach, max=reach).astype(kind)


def setup_inputs(seed: int = 0, part: int = 0) -> dict:
    splits = jax.random.split(jax.random.key(seed), 7)
    part_keys = jax.random.split(jax.random.fold_in(splits[6], part), 7)
    video = draw_video(jax.random.fold_in(jax.random.fold_in(splits[6], part), 71), part)
    w_in = noise(splits[1], (UNITS, 3), 3 ** -0.5, 3.5, jnp.float32)
    b_in = noise(splits[2], (UNITS,), 0.5, 2.0, jnp.float32)
    w_out = noise(splits[3], (3, UNITS), UNITS ** -0.5, 1.0, jnp.float32)
    b_out = noise(splits[4], (3,), 0.5, 2.0, jnp.float32)
    screen = jnp.clip(jnp.exp(jax.random.uniform(splits[5], (3,), jnp.float32, math.log(0.5), math.log(2.0))), 0.5, 2.0)
    return {"video": video, "w_in": w_in, "b_in": b_in, "w_out": w_out, "b_out": b_out, "screen": screen}


highest = lax.Precision.HIGHEST


def grade_frame(frame_in, w_in, b_in, w_out, b_out, screen):
    pixels = frame_in.astype(jnp.float32)
    before = jnp.einsum("jc,crw->jrw", w_in, pixels, precision=highest) + b_in[:, None, None]
    graded = pixels + jnp.einsum("cj,jrw->crw", w_out, jax.nn.silu(before), precision=highest) + b_out[:, None, None]
    padded = jnp.pad(graded, ((0, 0), (1, 1), (1, 1)))
    beside_all = padded[:, 2:, 1:-1] + padded[:, :-2, 1:-1] + padded[:, 1:-1, 2:] + padded[:, 1:-1, :-2]
    return ((screen[:, None, None] + 4.0) * graded - beside_all).astype(jnp.bfloat16)


def neighbours(padded):
    total = padded[2:, :, 1:-1, 1:-1] + padded[:-2, :, 1:-1, 1:-1]
    total = total + padded[1:-1, :, 2:, 1:-1] + padded[1:-1, :, :-2, 1:-1]
    total = total + padded[1:-1, :, 1:-1, 2:] + padded[1:-1, :, 1:-1, :-2]
    return total


def operate(field, screen):
    padded = jnp.pad(field, ((1, 1), (0, 0), (1, 1), (1, 1)))
    return (6.0 + screen[None, :, None, None]) * field - neighbours(padded)


def channel_dot(left, right):
    return jnp.sum(left * right, axis=(0, 2, 3))


def widen(values):
    return values[None, :, None, None]


def reference(video, w_in, b_in, w_out, b_out, screen):
    target = lax.map(lambda frame_in: grade_frame(frame_in, w_in, b_in, w_out, b_out, screen), video)
    source = target.astype(jnp.float32)
    solution = jnp.zeros_like(source)
    residual = source
    direction = source
    norm_now = channel_dot(residual, residual)
    for sweep_index in range(ITERS):
        image = operate(direction, screen)
        alpha = norm_now / channel_dot(direction, image)
        solution = solution + widen(alpha) * direction
        residual = residual - widen(alpha) * image
        norm_next = channel_dot(residual, residual)
        direction = residual + widen(norm_next / norm_now) * direction
        norm_now = norm_next
    return solution
```

```python
import jax
import jax.numpy as jnp
from jax import lax
from jax.sharding import PartitionSpec as P

highest = lax.Precision.HIGHEST


def grade_frame(frame_in, w_in, b_in, w_out, b_out, screen):
    pixels = frame_in.astype(jnp.float32)
    before = jnp.einsum("jc,crw->jrw", w_in, pixels, precision=highest) + b_in[:, None, None]
    graded = (
        pixels
        + jnp.einsum("cj,jrw->crw", w_out, jax.nn.silu(before), precision=highest)
        + b_out[:, None, None]
    )
    padded = jnp.pad(graded, ((0, 0), (1, 1), (1, 1)))
    beside_all = (
        padded[:, 2:, 1:-1] + padded[:, :-2, 1:-1] + padded[:, 1:-1, 2:] + padded[:, 1:-1, :-2]
    )
    return ((screen[:, None, None] + 4.0) * graded - beside_all).astype(jnp.bfloat16)


def shifted_sum(field, dim):
    widths = [(0, 0)] * field.ndim
    widths[dim] = (1, 1)
    padded = jnp.pad(field, widths)
    size = field.shape[dim]
    return lax.slice_in_dim(padded, 0, size, axis=dim) + lax.slice_in_dim(
        padded, 2, size + 2, axis=dim
    )


def within(field):
    return shifted_sum(field, 0) + shifted_sum(field, 3)


def dot(left, right):
    return jnp.sum(left * right, axis=(0, 2, 3))


def fifth(target):
    once = shifted_sum(target, 2)
    twice = shifted_sum(once, 2)
    return dot(twice, shifted_sum(twice, 2))


def with_halo(band, axis, width):
    count = lax.axis_size(axis)
    rows = band.shape[2]
    above = lax.ppermute(
        band[:, :, rows - width :], axis, [(i, i + 1) for i in range(count - 1)]
    )
    below = lax.ppermute(band[:, :, :width], axis, [(i + 1, i) for i in range(count - 1)])
    return jnp.concatenate([above, band, below], axis=2)


def everyone(values, axis):
    count = lax.axis_size(axis)
    copies = jnp.broadcast_to(values, (count,) + values.shape)
    return jnp.sum(lax.all_to_all(copies, axis, 0, 0), axis=0)


def galerkin(nu, sigma):
    g = [sigma * nu[k] - nu[k + 1] for k in range(5)]
    l1 = g[1] / g[0]
    l2 = g[2] / g[0]
    d1 = g[2] - l1 * g[1]
    e = g[3] - l1 * g[2]
    m = e / d1
    d2 = g[4] - l2 * g[2] - m * e
    z0 = nu[0]
    z1 = nu[1] - l1 * z0
    z2 = nu[2] - l2 * z0 - m * z1
    c2 = z2 / d2
    c1 = z1 / d1 - m * c2
    c0 = z0 / g[0] - l1 * c1 - l2 * c2
    return c0, c1, c2


def widen(values):
    return values[None, :, None, None]


def shards(video, w_in, b_in, w_out, b_out, screen):
    count, me = lax.axis_size("tm"), lax.axis_index("tm")
    target = lax.map(
        lambda frame_in: grade_frame(frame_in, w_in, b_in, w_out, b_out, screen), video
    )
    rho = fifth(target.astype(jnp.float32))
    band = lax.all_to_all(target, "tm", split_axis=2, concat_axis=0, tiled=True)
    rows = band.shape[2]
    held = with_halo(band, "tm", 2).astype(jnp.float32)
    row = me * rows - 1 + jnp.arange(rows + 2)
    inside = (row >= 0) & (row < count * rows)
    once = (held[:, :, 2:] + held[:, :, :-2]) * inside[None, None, :, None]
    u0 = held[:, :, 2:-2]
    u1 = once[:, :, 1:-1]
    u2 = once[:, :, 2:] + once[:, :, :-2]
    k0 = within(u0)
    k1 = within(u1)
    y = 2.0 * k1 + within(k0)
    y1 = 2.0 * within(u2) + within(k1)
    n1 = u1 + k0
    n2 = u2 + y
    last = dot(n2, within(n2)) + dot(y, y1) + 2.0 * dot(y1, u2) + rho
    nu = jnp.stack([dot(u0, u0), dot(u0, n1), dot(n1, n1), dot(n1, n2), dot(n2, n2), last])
    nu = everyone(nu, "tm")
    c0, c1, c2 = galerkin(nu, 6.0 + screen)
    return widen(c0) * u0 + widen(c1) * n1 + widen(c2) * n2


def solution(mesh):
    in_specs = (P(("video", "tm"), None, None, None), P(), P(), P(), P(), P())
    out_specs = P("video", None, "tm", None)
    return jax.shard_map(shards, mesh=mesh, in_specs=in_specs, out_specs=out_specs, check_vma=False)
```

```python
import functools

import jax
import jax.numpy as jnp
from jax import lax
from jax.experimental import pallas as pl
from jax.experimental.pallas import tpu as pltpu
from jax.sharding import PartitionSpec as P

BLOCKS = 8
LANES = 128
AXIS = "tm"


def lanes_of(shape):
    return lax.broadcasted_iota(jnp.int32, shape, len(shape) - 1)


def grade_kernel(w_in, b_in, w_out, b_out, screen, video, chunks, rho, padded, graded, blocks):
    channels, rows, columns = video.shape[1:]
    units = w_in.shape[0]
    across = padded.shape[2]
    width = columns // BLOCKS
    halo = (LANES - width) // 2
    dests = chunks.shape[0]

    for c in range(channels):
        padded[c, :, :] = jnp.zeros((rows, across), jnp.float32)
        padded[c, :, :columns] = video[0, c].astype(jnp.float32)

    def grade(step, _):
        at = pl.ds(pl.multiple_of(step * LANES, LANES), LANES)
        pixels = [padded[c, :, at] for c in range(channels)]
        total = [pixels[c] + b_out[c] for c in range(channels)]
        for j in range(units):
            half = pixels[0] * (0.5 * w_in[j, 0])
            for c in range(1, channels):
                half = half + pixels[c] * (0.5 * w_in[j, c])
            half = half + 0.5 * b_in[j]
            unit = half + half * jnp.tanh(half)
            for c in range(channels):
                total[c] = total[c] + w_out[c, j] * unit
        inside = step * LANES + lanes_of((rows, LANES)) < columns
        for c in range(channels):
            graded[c, :, at] = jnp.where(inside, total[c], 0.0)
        return 0

    lax.fori_loop(0, across // LANES, grade, 0)

    row = lax.broadcasted_iota(jnp.int32, (rows, across), 0)
    lane = lanes_of((8, LANES))
    for c in range(channels):
        g = graded[c]
        above = jnp.where(row == 0, 0.0, pltpu.roll(g, 1, 0))
        below = jnp.where(row == rows - 1, 0.0, pltpu.roll(g, rows - 1, 0))
        beside = pltpu.roll(g, 1, 1) + pltpu.roll(g, across - 1, 1)
        target = (screen[c] + 4.0) * g - (above + below + beside)
        inside = lanes_of((rows, across)) < columns
        target = jnp.where(inside, target, 0.0).astype(jnp.bfloat16).astype(jnp.float32)
        for first in range(0, rows, 8):
            tile = target[first : first + 8]
            parts = []
            for s in range(BLOCKS):
                start = s * width - halo
                v, off = start // LANES, start % LANES
                low = jnp.zeros((8, LANES), jnp.float32)
                if v >= 0:
                    low = pltpu.roll(tile[:, v * LANES : (v + 1) * LANES], (LANES - off) % LANES, 1)
                high = pltpu.roll(tile[:, (v + 1) * LANES : (v + 2) * LANES], LANES - off, 1)
                parts.append(jnp.where(lane < LANES - off, low, high))
            blocks[c, first : first + 8] = jnp.swapaxes(jnp.stack(parts, axis=0), 0, 1)

    for c in range(channels):
        field = [blocks[c, r] for r in range(rows)]
        for _ in range(2):
            field = [
                sum(field[i] for i in (r - 1, r + 1) if 0 <= i < rows) for r in range(rows)
            ]
        total = field[0] * field[1]
        for r in range(1, rows - 1):
            total = total + field[r] * field[r + 1]
        rho[c] = total + total
        zero = jnp.zeros((BLOCKS, LANES), jnp.float32)

        def line(r):
            return blocks[c, r] if 0 <= r < rows else zero

        for d in range(dests):
            if d % 2 == 0:
                order = [2 * d - 2, 2 * d - 1, 2 * d, 2 * d + 1]
            else:
                order = [2 * d + 3, 2 * d + 2, 2 * d + 1, 2 * d]
            for p in range(2):
                pair = jnp.concatenate([line(order[2 * p]), line(order[2 * p + 1])], axis=0)
                chunks[d, p, c] = pair.astype(jnp.bfloat16)


def within(field, mask):
    zero = jnp.zeros_like(field[:1])
    frames = jnp.concatenate([field[1:], zero], axis=0) + jnp.concatenate([zero, field[:-1]], axis=0)
    beside = pltpu.roll(field, 1, 2) + pltpu.roll(field, LANES - 1, 2)
    return frames + jnp.where(mask, beside, 0.0)


def moment_kernel(columns, edge, held, sibling, rho, sums, first, second):
    frames, _, channels = held.shape[:3]
    width = columns // BLOCKS
    halo = (LANES - width) // 2
    shape = (frames, 2 * BLOCKS, LANES)
    lane = lanes_of(shape)
    column = (lax.broadcasted_iota(jnp.int32, shape, 1) % BLOCKS) * width - halo + lane
    mask = (column >= 0) & (column < columns)
    own = lanes_of((2 * BLOCKS, LANES))
    own = (own >= halo) & (own < halo + width)
    inside = edge[0]
    out_lane = lanes_of((1, LANES))
    result = jnp.zeros((1, LANES), jnp.float32)
    for c in range(channels):
        far = held[:, 0, c].astype(jnp.float32)
        u0 = held[:, 1, c].astype(jnp.float32)
        near = sibling[:, c].astype(jnp.float32)
        b0, b1 = far[:, :BLOCKS], far[:, BLOCKS:]
        b2, b3 = u0[:, :BLOCKS], u0[:, BLOCKS:]
        b5, b4 = near[:, :BLOCKS], near[:, BLOCKS:]
        u1 = jnp.concatenate([b1 + b3, b2 + b4], axis=1)
        u2 = jnp.concatenate([b0 + (1.0 + inside) * b2 + b4, b1 + 2.0 * b3 + b5], axis=1)
        k0 = within(u0, mask)
        k1 = within(u1, mask)
        y = 2.0 * k1 + within(k0, mask)
        y1 = 2.0 * within(u2, mask) + within(k1, mask)
        n1 = u1 + k0
        n2 = u2 + y
        first[c] = n1
        second[c] = n2
        moments = [
            u0 * u0,
            u0 * n1,
            n1 * n1,
            n1 * n2,
            n2 * n2,
            n2 * within(n2, mask) + y * y1 + 2.0 * (y1 * u2),
        ]
        for k, product in enumerate(moments):
            total = jnp.sum(product, axis=0)
            total = total[:BLOCKS] + total[BLOCKS:]
            if k == len(moments) - 1:
                total = total + rho[c]
            total = jnp.where(own[:BLOCKS], total, 0.0)
            total = jnp.sum(total, axis=0, keepdims=True)
            total = jnp.sum(total, axis=1, keepdims=True)
            result = jnp.where(out_lane == BLOCKS * k + c, total, result)
    sums[...] = jnp.broadcast_to(result[None], sums.shape)


def combine_kernel(columns, screen, sums, held, first, second, out):
    frames, _, channels = held.shape[:3]
    width = columns // BLOCKS
    halo = (LANES - width) // 2
    lane = lanes_of((1, LANES))
    total = jnp.sum(sums[...], axis=0)
    nu = [total] + [pltpu.roll(total, LANES - BLOCKS * k, 1) for k in range(1, 6)]
    sigma = jnp.full((1, LANES), 1.0, jnp.float32)
    for c in range(channels):
        sigma = jnp.where(lane == c, 6.0 + screen[c], sigma)
    g = [sigma * nu[k] - nu[k + 1] for k in range(5)]
    l1 = g[1] / g[0]
    l2 = g[2] / g[0]
    d1 = g[2] - l1 * g[1]
    e = g[3] - l1 * g[2]
    m = e / d1
    d2 = g[4] - l2 * g[2] - m * e
    z0 = nu[0]
    z1 = nu[1] - l1 * z0
    z2 = nu[2] - l2 * z0 - m * z1
    c2 = z2 / d2
    c1 = z1 / d1 - m * c2
    c0 = z0 / g[0] - l1 * c1 - l2 * c2

    tile_lane = lanes_of((8, LANES))
    tiles = -(-columns // LANES)
    for c in range(channels):
        w0, w1, w2 = (
            jnp.sum(jnp.where(lane == c, w, 0.0), axis=1, keepdims=True)[None] for w in (c0, c1, c2)
        )
        for row in range(2):
            part = slice(row * BLOCKS, (row + 1) * BLOCKS)
            x = (
                w0 * held[:, 1, c, part].astype(jnp.float32)
                + w1 * first[c, :, part]
                + w2 * second[c, :, part]
            )
            for f in range(0, frames, 8):
                turned = jnp.swapaxes(x[f : f + 8], 0, 1)
                moved = [
                    pltpu.roll(turned[s], (s * width - halo) % LANES, 1) for s in range(BLOCKS)
                ]
                for t in range(tiles):
                    bound = width * (t + 1) - LANES * t
                    piece = moved[t]
                    if t + 1 < BLOCKS:
                        piece = jnp.where(tile_lane < bound, moved[t], moved[t + 1])
                    count = min(LANES, columns - LANES * t)
                    out[c, row, f : f + 8, LANES * t : LANES * t + count] = piece[:, :count]


def smem():
    return pl.BlockSpec(memory_space=pltpu.SMEM)


def vmem():
    return pl.BlockSpec(memory_space=pltpu.VMEM)


def shards(video, w_in, b_in, w_out, b_out, screen):
    count, me = lax.axis_size(AXIS), lax.axis_index(AXIS)
    _, channels, rows, columns = video.shape
    frames = count
    across = -(-columns // LANES) * LANES
    chunks, rho = pl.pallas_call(
        grade_kernel,
        out_shape=(
            jax.ShapeDtypeStruct((count, 2, channels, 2 * BLOCKS, LANES), jnp.bfloat16),
            jax.ShapeDtypeStruct((channels, BLOCKS, LANES), jnp.float32),
        ),
        in_specs=[smem()] * 5 + [vmem()],
        out_specs=(vmem(), vmem()),
        scratch_shapes=[
            pltpu.VMEM((channels, rows, across), jnp.float32),
            pltpu.VMEM((channels, rows, across), jnp.float32),
            pltpu.VMEM((channels, rows, BLOCKS, LANES), jnp.float32),
        ],
        name="grade",
    )(w_in, b_in, w_out, b_out, screen, video)
    held = lax.all_to_all(chunks, AXIS, 0, 0)
    sibling = lax.ppermute(held[:, 1], AXIS, [(i, i ^ 1) for i in range(count)])
    edge = jnp.where((me == 0) | (me == count - 1), 0.0, 1.0).reshape(1)
    field = jax.ShapeDtypeStruct((channels, frames, 2 * BLOCKS, LANES), jnp.float32)
    sums, first, second = pl.pallas_call(
        functools.partial(moment_kernel, columns),
        out_shape=(jax.ShapeDtypeStruct((count, 1, LANES), jnp.float32), field, field),
        in_specs=[smem()] + [vmem()] * 3,
        out_specs=(vmem(),) * 3,
        name="moments",
    )(edge, held, sibling, rho)
    sums = lax.all_to_all(sums, AXIS, 0, 0)
    out = pl.pallas_call(
        functools.partial(combine_kernel, columns),
        out_shape=jax.ShapeDtypeStruct((channels, 2, frames, columns), jnp.float32),
        in_specs=[smem()] + [vmem()] * 4,
        out_specs=vmem(),
        name="combine",
    )(screen, sums, held, first, second)
    out = jnp.where(me % 2 == 0, out, out[:, ::-1])
    return out.transpose(2, 0, 1, 3)


def solution(mesh):
    in_specs = (P(("video", AXIS), None, None, None), P(), P(), P(), P(), P())
    out_specs = P("video", None, AXIS, None)
    return jax.shard_map(shards, mesh=mesh, in_specs=in_specs, out_specs=out_specs, check_vma=False)
```

```python
import functools

import jax
import jax.numpy as jnp
from jax import lax
from jax.experimental import pallas as pl
from jax.experimental.pallas import tpu as pltpu
from jax.sharding import PartitionSpec as P

BLOCKS = 8
LANES = 128
AXIS = "tm"


def lanes_of(shape):
    return lax.broadcasted_iota(jnp.int32, shape, len(shape) - 1)


def three_parts(values, lane):
    high = values.astype(jnp.bfloat16).astype(jnp.float32)
    rest = values - high
    middle = rest.astype(jnp.bfloat16).astype(jnp.float32)
    third = LANES // 4
    return jnp.where(lane < third, high, jnp.where(lane < 2 * third, middle, rest - middle))


def grade_kernel(
    w_in_at, b_in_at, w_out_at, b_out_at, screen_at, video_at, chunks, rho, sigma,
    w_in, b_in, w_out, b_out, screen, video, arrived, graded, blocks, first, second,
):
    copies = [
        pltpu.make_async_copy(source, to, arrived.at[i])
        for i, (source, to) in enumerate(
            [
                (w_in_at, w_in), (b_in_at, b_in), (w_out_at, w_out),
                (b_out_at, b_out), (screen_at, screen), (video_at, video),
            ]
        )
    ]
    for copy in copies:
        copy.start()
    for copy in copies:
        copy.wait()
    channels, rows, columns = video.shape[1:]
    units = b_in.shape[0]
    across = graded.shape[2]
    width = columns // BLOCKS
    halo = (LANES - width) // 2
    dests = chunks.shape[0]

    tile = (8, LANES)
    lane = lanes_of(tile)
    part = lane % (LANES // 4)
    row = lax.broadcasted_iota(jnp.int32, tile, 0)
    used = lane < 3 * (LANES // 4)
    picks = [jnp.where(used & (part == 8 * c + row), 0.5, 0.0) for c in range(channels)]
    ones = jnp.where(used & (part == 8 * channels), 0.5, 0.0)
    for j in range(units):
        values = ones * b_in[j]
        for c in range(channels):
            values = values + picks[c] * w_in[c, j]
            second[c, j] = jnp.full(tile, w_out[c, j])
        first[8 * j : 8 * j + 8] = three_parts(values, lane)
    layer = first[...].astype(jnp.bfloat16)

    span = across // 2

    def grade(step, _):
        top = pl.multiple_of(step * 16, 16)
        for start in range(0, across, span):
            count = min(span, columns - start)
            taken = []
            for c in range(channels):
                values = video[0, c, pl.ds(top, 16), start : start + count].astype(jnp.float32)
                if count < span:
                    empty = jnp.zeros((16, span - count), jnp.float32)
                    values = jnp.concatenate([values, empty], axis=1)
                taken.append(values)
            for r in (0, 8):
                pixels = [values[r : r + 8] for values in taken]
                group = jnp.concatenate(pixels + [jnp.ones((8, span), jnp.float32)], axis=0)
                group = group.astype(jnp.bfloat16)
                group = jnp.concatenate([group] * 3 + [jnp.zeros_like(group)], axis=0)
                half = jnp.dot(layer, group, preferred_element_type=jnp.float32)
                total = [pixels[c] + b_out[c] for c in range(channels)]
                for j in range(units):
                    h = half[8 * j : 8 * j + 8]
                    unit = h + h * jnp.tanh(h)
                    for c in range(channels):
                        total[c] = total[c] + jnp.tile(second[c, j], (1, span // LANES)) * unit
                inside = start + lanes_of((8, span)) < columns
                for c in range(channels):
                    graded[c, pl.ds(top + r, 8), start : start + span] = jnp.where(
                        inside, total[c], 0.0
                    )
        return 0

    lax.fori_loop(0, rows // 16, grade, 0)

    row = lax.broadcasted_iota(jnp.int32, (rows, across), 0)
    inside = lanes_of((rows, across)) < columns
    weight = jnp.full((1, LANES), 1.0, jnp.float32)
    for c in range(channels):
        weight = jnp.where(lane[:1] == c, 6.0 + screen[c], weight)
        g = graded[c]
        above = jnp.where(row == 0, 0.0, pltpu.roll(g, 1, 0))
        below = jnp.where(row == rows - 1, 0.0, pltpu.roll(g, rows - 1, 0))
        beside = pltpu.roll(g, 1, 1) + pltpu.roll(g, across - 1, 1)
        target = (screen[c] + 4.0) * g - (above + below + beside)
        target = jnp.where(inside, target, 0.0).astype(jnp.bfloat16).astype(jnp.float32)
        for top in range(0, rows, 8):
            band = target[top : top + 8]
            parts = []
            for s in range(BLOCKS):
                start = s * width - halo
                v, off = start // LANES, start % LANES
                low = jnp.zeros(tile, jnp.float32)
                if v >= 0:
                    low = pltpu.roll(band[:, v * LANES : (v + 1) * LANES], (LANES - off) % LANES, 1)
                high = pltpu.roll(band[:, (v + 1) * LANES : (v + 2) * LANES], LANES - off, 1)
                parts.append(jnp.where(lane < LANES - off, low, high))
            blocks[c, top : top + 8] = jnp.swapaxes(jnp.stack(parts, axis=0), 0, 1)
    sigma[...] = weight

    for c in range(channels):
        field = [blocks[c, r] for r in range(rows)]
        for _ in range(2):
            field = [
                sum(field[i] for i in (r - 1, r + 1) if 0 <= i < rows) for r in range(rows)
            ]
        total = field[0] * field[1]
        for r in range(1, rows - 1):
            total = total + field[r] * field[r + 1]
        rho[c] = total + total
        zero = jnp.zeros((BLOCKS, LANES), jnp.float32)

        def line(r):
            return blocks[c, r] if 0 <= r < rows else zero

        for d in range(dests):
            if d % 2 == 0:
                order = [2 * d - 2, 2 * d - 1, 2 * d, 2 * d + 1]
            else:
                order = [2 * d + 3, 2 * d + 2, 2 * d + 1, 2 * d]
            for p in range(2):
                pair = jnp.concatenate([line(order[2 * p]), line(order[2 * p + 1])], axis=0)
                chunks[d, p, c] = pair.astype(jnp.bfloat16)


def within(field, mask):
    zero = jnp.zeros_like(field[:1])
    frames = jnp.concatenate([field[1:], zero], axis=0) + jnp.concatenate([zero, field[:-1]], axis=0)
    beside = pltpu.roll(field, 1, 2) + pltpu.roll(field, LANES - 1, 2)
    return frames + jnp.where(mask, beside, 0.0)


def moment_kernel(columns, place, held, sibling, rho, sums, first, second):
    frames, _, channels = held.shape[:3]
    width = columns // BLOCKS
    halo = (LANES - width) // 2
    shape = (frames, 2 * BLOCKS, LANES)
    lane = lanes_of(shape)
    column = (lax.broadcasted_iota(jnp.int32, shape, 1) % BLOCKS) * width - halo + lane
    mask = (column >= 0) & (column < columns)
    own = lanes_of((2 * BLOCKS, LANES))
    own = (own >= halo) & (own < halo + width)
    inside = place[0]
    out_lane = lanes_of((1, LANES))
    result = jnp.zeros((1, LANES), jnp.float32)
    for c in range(channels):
        far = held[:, 0, c].astype(jnp.float32)
        u0 = held[:, 1, c].astype(jnp.float32)
        near = sibling[:, c].astype(jnp.float32)
        b0, b1 = far[:, :BLOCKS], far[:, BLOCKS:]
        b2, b3 = u0[:, :BLOCKS], u0[:, BLOCKS:]
        b5, b4 = near[:, :BLOCKS], near[:, BLOCKS:]
        u1 = jnp.concatenate([b1 + b3, b2 + b4], axis=1)
        u2 = jnp.concatenate([b0 + inside * b2 + b4, b1 + 2.0 * b3 + b5], axis=1)
        k0 = within(u0, mask)
        k1 = within(u1, mask)
        y = 2.0 * k1 + within(k0, mask)
        y1 = 2.0 * within(u2, mask) + within(k1, mask)
        n1 = u1 + k0
        n2 = u2 + y
        first[c] = n1
        second[c] = n2
        moments = [
            u0 * u0,
            u0 * n1,
            n1 * n1,
            n1 * n2,
            n2 * n2,
            n2 * within(n2, mask) + y * y1 + 2.0 * (y1 * u2),
        ]
        for k, product in enumerate(moments):
            total = jnp.sum(product, axis=0)
            total = total[:BLOCKS] + total[BLOCKS:]
            if k == len(moments) - 1:
                total = total + rho[c]
            total = jnp.where(own[:BLOCKS], total, 0.0)
            total = jnp.sum(total, axis=0, keepdims=True)
            total = jnp.sum(total, axis=1, keepdims=True)
            result = jnp.where(out_lane == BLOCKS * k + c, total, result)
    sums[...] = jnp.broadcast_to(result[None], sums.shape)


def combine_kernel(columns, place, sigma_at, sums, held, first, second, out):
    frames, _, channels = held.shape[:3]
    width = columns // BLOCKS
    halo = (LANES - width) // 2
    lane = lanes_of((1, LANES))
    total = jnp.sum(sums[...], axis=0)
    nu = [total] + [pltpu.roll(total, LANES - BLOCKS * k, 1) for k in range(1, 6)]
    sigma = sigma_at[...]
    g = [sigma * nu[k] - nu[k + 1] for k in range(5)]
    l1 = g[1] / g[0]
    l2 = g[2] / g[0]
    d1 = g[2] - l1 * g[1]
    e = g[3] - l1 * g[2]
    m = e / d1
    d2 = g[4] - l2 * g[2] - m * e
    z0 = nu[0]
    z1 = nu[1] - l1 * z0
    z2 = nu[2] - l2 * z0 - m * z1
    c2 = z2 / d2
    c1 = z1 / d1 - m * c2
    c0 = z0 / g[0] - l1 * c1 - l2 * c2

    tile_lane = lanes_of((8, LANES))
    tiles = -(-columns // LANES)
    mirrored = place[1] > 0.5
    for c in range(channels):
        w0, w1, w2 = (
            jnp.sum(jnp.where(lane == c, w, 0.0), axis=1, keepdims=True)[None] for w in (c0, c1, c2)
        )
        x = w0 * held[:, 1, c].astype(jnp.float32) + w1 * first[c] + w2 * second[c]
        low, high = x[:, :BLOCKS], x[:, BLOCKS:]
        low, high = jnp.where(mirrored, high, low), jnp.where(mirrored, low, high)
        for f in range(0, frames, 4):
            lines = [part[i] for i in range(f, f + 4) for part in (low, high)]
            turned = jnp.swapaxes(jnp.stack(lines, axis=0), 0, 1)
            moved = [pltpu.roll(turned[s], (s * width - halo) % LANES, 1) for s in range(BLOCKS)]
            for t in range(tiles):
                piece = moved[t]
                if t + 1 < BLOCKS:
                    bound = width * (t + 1) - LANES * t
                    piece = jnp.where(tile_lane < bound, moved[t], moved[t + 1])
                count = min(LANES, columns - LANES * t)
                for i in range(4):
                    out[f + i, c, :, LANES * t : LANES * t + count] = piece[
                        2 * i : 2 * i + 2, :count
                    ]


def vmem():
    return pl.BlockSpec(memory_space=pltpu.VMEM)


def params():
    return pltpu.CompilerParams(vmem_limit_bytes=32 << 20)


def shards(video, w_in, b_in, w_out, b_out, screen):
    count, me = lax.axis_size(AXIS), lax.axis_index(AXIS)
    _, channels, rows, columns = video.shape
    units = b_in.shape[0]
    frames = count
    across = -(-columns // LANES) * LANES
    w_in = w_in.T
    operands = (w_in, b_in, w_out, b_out, screen, video)
    local = [pltpu.SMEM(a.shape, a.dtype) for a in operands[:-1]]
    chunks, rho, sigma = pl.pallas_call(
        grade_kernel,
        out_shape=(
            jax.ShapeDtypeStruct((count, 2, channels, 2 * BLOCKS, LANES), jnp.bfloat16),
            jax.ShapeDtypeStruct((channels, BLOCKS, LANES), jnp.float32),
            jax.ShapeDtypeStruct((1, LANES), jnp.float32),
        ),
        in_specs=[pl.BlockSpec(memory_space=pltpu.HBM)] * 6,
        out_specs=(vmem(),) * 3,
        scratch_shapes=local
        + [
            pltpu.VMEM(video.shape, video.dtype),
            pltpu.SemaphoreType.DMA((6,)),
            pltpu.VMEM((channels, rows, across), jnp.float32),
            pltpu.VMEM((channels, rows, BLOCKS, LANES), jnp.float32),
            pltpu.VMEM((8 * units, LANES), jnp.float32),
            pltpu.VMEM((channels, units, 8, LANES), jnp.float32),
        ],
        name="grade",
    )(*operands)
    held = lax.all_to_all(chunks, AXIS, 0, 0)
    sibling = lax.ppermute(held[:, 1], AXIS, [(i, i ^ 1) for i in range(count)])
    inside = jnp.where((me == 0) | (me == count - 1), 1.0, 2.0)
    odd = jnp.where(me % 2 == 1, 1.0, 0.0)
    place = jnp.broadcast_to(jnp.stack([inside, odd])[:, None, None], (2, BLOCKS, LANES))
    field = jax.ShapeDtypeStruct((channels, frames, 2 * BLOCKS, LANES), jnp.float32)
    sums, first, second = pl.pallas_call(
        functools.partial(moment_kernel, columns),
        out_shape=(jax.ShapeDtypeStruct((count, 1, LANES), jnp.float32), field, field),
        in_specs=[vmem()] * 4,
        out_specs=(vmem(),) * 3,
        compiler_params=params(),
        name="moments",
    )(place, held, sibling, rho)
    sums = lax.all_to_all(sums, AXIS, 0, 0)
    return pl.pallas_call(
        functools.partial(combine_kernel, columns),
        out_shape=jax.ShapeDtypeStruct((frames, channels, 2, columns), jnp.float32),
        in_specs=[vmem()] * 6,
        out_specs=vmem(),
        compiler_params=params(),
        name="combine",
    )(place, sigma, sums, held, first, second)


def solution(mesh):
    in_specs = (P(("video", AXIS), None, None, None), P(), P(), P(), P(), P())
    out_specs = P("video", None, AXIS, None)
    return jax.shard_map(shards, mesh=mesh, in_specs=in_specs, out_specs=out_specs, check_vma=False)
```

```python
import functools

import jax
import jax.numpy as jnp
from jax import lax
from jax.experimental import pallas as pl
from jax.experimental.pallas import tpu as pltpu
from jax.sharding import PartitionSpec as P

BLOCKS = 8
LANES = 128
TILE = (8, LANES)
AXIS = "tm"


def lanes_of(shape):
    return lax.broadcasted_iota(jnp.int32, shape, len(shape) - 1)


def sublanes_of(shape):
    return lax.broadcasted_iota(jnp.int32, shape, len(shape) - 2)


def turn_pairs(tiles):
    sublane = sublanes_of(TILE)
    lower, even = sublane < 4, sublane % 4 < 2
    mixed = []
    for i in (0, 1):
        a, b = tiles[i], tiles[i + 2]
        mixed.append(
            (jnp.where(lower, a, pltpu.roll(b, 4, 0)), jnp.where(lower, pltpu.roll(a, 4, 0), b))
        )
    turned = []
    for i in (0, 1):
        a, b = mixed[0][i], mixed[1][i]
        turned.append(jnp.where(even, a, pltpu.roll(b, 2, 0)))
        turned.append(jnp.where(even, pltpu.roll(a, 6, 0), b))
    return turned


def three_parts(values, lane):
    high = values.astype(jnp.bfloat16).astype(jnp.float32)
    rest = values - high
    middle = rest.astype(jnp.bfloat16).astype(jnp.float32)
    third = LANES // 4
    return jnp.where(lane < third, high, jnp.where(lane < 2 * third, middle, rest - middle))


def grade_kernel(
    w_in_at, b_in_at, w_out_at, b_out_at, screen_at, video_at, chunks, extra,
    w_in, b_in, w_out, b_out, screen, video, arrived, sent,
    graded, tiles, first, second, ready, notes,
):
    channels, rows, columns = video.shape[1:]
    units = b_in.shape[0]
    across = graded.shape[2]
    width = columns // BLOCKS
    halo = (LANES - width) // 2
    chips = chunks.shape[0] // 2
    weights = [
        pltpu.make_async_copy(source, to, arrived.at[i])
        for i, (source, to) in enumerate(
            [
                (w_in_at, w_in), (b_in_at, b_in), (w_out_at, w_out),
                (b_out_at, b_out), (screen_at, screen),
            ]
        )
    ]
    pixels_in = pltpu.make_async_copy(video_at, video, arrived.at[5])
    pixels_in.start()
    for copy in weights:
        copy.start()
    for copy in weights:
        copy.wait()

    lane, sublane = lanes_of(TILE), sublanes_of(TILE)
    part = lane % (LANES // 4)
    used = lane < 3 * (LANES // 4)
    picks = [jnp.where(used & (part == 8 * c + sublane), 0.5, 0.0) for c in range(channels)]
    ones = jnp.where(used & (part == 8 * channels), 0.5, 0.0)
    mix = [[jnp.zeros(TILE, jnp.float32) for _ in range(channels + 1)] for _ in range(channels)]
    for j in range(units):
        into = [jnp.full(TILE, w_in[c, j]) for c in range(channels)] + [jnp.full(TILE, b_in[j])]
        values = ones * into[channels]
        for c in range(channels):
            values = values + picks[c] * into[c]
        first[8 * j : 8 * j + 8] = three_parts(values, lane)
        for c in range(channels):
            out = jnp.full(TILE, w_out[c, j])
            second[c, j] = out
            for k in range(channels + 1):
                mix[c][k] = mix[c][k] + (0.5 * out) * into[k]
    for c in range(channels):
        mix[c][c] = mix[c][c] + 1.0
        mix[c][channels] = mix[c][channels] + b_out[c]
    layer = first[...].astype(jnp.bfloat16)
    pixels_in.wait()

    span = across // 2
    times = span // LANES

    def wide(tile):
        return jnp.tile(tile, (1, times))

    def grade(step, _):
        top = pl.multiple_of(step * 16, 16)
        for start in range(0, across, span):
            count = min(span, columns - start)
            taken = []
            for c in range(channels):
                values = video[0, c, pl.ds(top, 16), start : start + count].astype(jnp.float32)
                if count < span:
                    empty = jnp.zeros((16, span - count), jnp.float32)
                    values = jnp.concatenate([values, empty], axis=1)
                taken.append(values)
            for r in (0, 8):
                pixels = [values[r : r + 8] for values in taken]
                group = jnp.concatenate(pixels + [jnp.ones((8, span), jnp.float32)], axis=0)
                group = group.astype(jnp.bfloat16)
                group = jnp.concatenate([group] * 3 + [jnp.zeros_like(group)], axis=0)
                half = jnp.dot(layer, group, preferred_element_type=jnp.float32)
                total = []
                for c in range(channels):
                    linear = wide(mix[c][channels])
                    for k in range(channels):
                        linear = linear + wide(mix[c][k]) * pixels[k]
                    total.append(linear)
                for j in range(units):
                    h = half[8 * j : 8 * j + 8]
                    unit = h * jnp.tanh(h)
                    for c in range(channels):
                        total[c] = total[c] + wide(second[c, j]) * unit
                inside = start + lanes_of((8, span)) < columns
                for c in range(channels):
                    graded[c, pl.ds(top + r, 8), start : start + span] = jnp.where(
                        inside, total[c], 0.0
                    )
        return 0

    lax.fori_loop(0, rows // 16, grade, 0)

    line = sublanes_of((rows, across))
    inside = lanes_of((rows, across)) < columns
    upper = sublane % 2 == 0
    zero = jnp.zeros(TILE, jnp.float32)
    sigma = jnp.full(TILE, 1.0, jnp.float32)
    copies = []
    for c in range(channels):
        sigma = jnp.where(lane == c, 6.0 + screen[c], sigma)
        g = graded[c]
        above = jnp.where(line == 0, 0.0, pltpu.roll(g, 1, 0))
        below = jnp.where(line == rows - 1, 0.0, pltpu.roll(g, rows - 1, 0))
        beside = pltpu.roll(g, 1, 1) + pltpu.roll(g, across - 1, 1)
        target = (screen[c] + 4.0) * g - (above + below + beside)
        target = jnp.where(inside, target, 0.0).astype(jnp.bfloat16).astype(jnp.float32)
        for top in range(0, rows, 8):
            band = target[top : top + 8]
            parts = []
            for s in range(BLOCKS):
                start = s * width - halo
                v, off = start // LANES, start % LANES
                low = zero
                if v >= 0:
                    low = pltpu.roll(band[:, v * LANES : (v + 1) * LANES], (LANES - off) % LANES, 1)
                high = pltpu.roll(band[:, (v + 1) * LANES : (v + 2) * LANES], LANES - off, 1)
                parts.append(jnp.where(lane < LANES - off, low, high))
            for side in range(2):
                for k, tile in enumerate(turn_pairs(parts[4 * side : 4 * side + 4])):
                    tiles[c, side, top // 2 + k] = tile
        pairs = rows // 2
        for side in range(2):

            def pair(k):
                return tiles[c, side, k] if 0 <= k < pairs else zero

            for q in range(chips):
                for p in range(2):
                    k = 2 * q - 1 + 2 * p
                    both = jnp.concatenate([pair(k), pair(k + 1)], axis=0)
                    ready[c, 2 * q + side, p] = both.astype(jnp.bfloat16)
        copies.append(pltpu.make_async_copy(ready.at[c], chunks.at[:, c], sent.at[c]))
        copies[-1].start()

    for c in range(channels):
        total = zero
        for side in range(2):
            field = [tiles[c, side, k] for k in range(pairs)]
            twice = []
            for k in range(pairs):
                beyond = zero
                if k > 0:
                    beyond = beyond + field[k - 1]
                if k < pairs - 1:
                    beyond = beyond + field[k + 1]
                own = 2.0 * field[k]
                if k == 0:
                    own = jnp.where(upper, field[k], own)
                if k == pairs - 1:
                    own = jnp.where(upper, own, field[k])
                twice.append(own + beyond)
            for k in range(pairs):
                after = pltpu.roll(twice[k + 1], 1, 0) if k < pairs - 1 else zero
                total = total + twice[k] * jnp.where(upper, pltpu.roll(twice[k], 7, 0), after)
        notes[c] = total + total
    notes[channels] = sigma
    copies.append(pltpu.make_async_copy(notes, extra, sent.at[channels]))
    copies[-1].start()
    for copy in copies:
        copy.wait()


def within(field, mask):
    zero = jnp.zeros_like(field[:1])
    frames = jnp.concatenate([field[1:], zero], axis=0) + jnp.concatenate([zero, field[:-1]], axis=0)
    beside = pltpu.roll(field, 1, 2) + pltpu.roll(field, LANES - 1, 2)
    return frames + jnp.where(mask, beside, 0.0)


def moment_kernel(columns, place, held, extra, sums, kept, given, sigma):
    frames, channels = held.shape[:2]
    width = columns // BLOCKS
    halo = (LANES - width) // 2
    odd = place[2] > 0.5
    lane, sublane = lanes_of(TILE), sublanes_of(TILE)
    block = sublane // 2 + jnp.where(odd, BLOCKS // 2, 0)
    column = block * width - halo + lane
    mask = ((column >= 0) & (column < columns))[None]
    own = (lane >= halo) & (lane < halo + width)
    upper = (sublane % 2 == 0)[None]
    top = jnp.where(upper, place[0][None], 2.0)
    bottom = jnp.where(upper, 2.0, place[1][None])
    out_lane = lanes_of((1, LANES))
    result = jnp.zeros((1, LANES), jnp.float32)
    for c in range(channels):
        halves = [held[:, c, p].astype(jnp.float32) for p in range(2)]
        b = [halves[0][:, :8], halves[0][:, 8:], halves[1][:, :8], halves[1][:, 8:]]
        between = [b[i] + b[i + 1] for i in range(3)]
        totals = [jnp.zeros(TILE, jnp.float32) for _ in range(6)]
        totals[5] = extra[c]
        sides = []
        for i in (1, 2):
            u0 = b[i]
            u1 = jnp.where(upper, pltpu.roll(between[i - 1], 7, 1), pltpu.roll(between[i], 1, 1))
            u2 = b[i - 1] + (top if i == 1 else bottom) * u0 + b[i + 1]
            k0 = within(u0, mask)
            k1 = within(u1, mask)
            y = 2.0 * k1 + within(k0, mask)
            y1 = 2.0 * within(u2, mask) + within(k1, mask)
            n1 = u1 + k0
            n2 = u2 + y
            sides.append((u0, n1, n2))
            products = [
                u0 * u0,
                u0 * n1,
                n1 * n1,
                n1 * n2,
                n2 * n2,
                n2 * within(n2, mask) + y * y1 + 2.0 * (y1 * u2),
            ]
            for k, product in enumerate(products):
                totals[k] = totals[k] + jnp.sum(product, axis=0)
        for k in range(3):
            kept[k, c] = jnp.where(odd[None], sides[1][k], sides[0][k])
            given[k, c] = jnp.where(odd[None], sides[0][k], sides[1][k])
        for k, total in enumerate(totals):
            total = jnp.where(own, total, 0.0)
            total = jnp.sum(total, axis=0, keepdims=True)
            total = jnp.sum(total, axis=1, keepdims=True)
            result = jnp.where(out_lane == 8 * k + c, total, result)
    sums[...] = jnp.broadcast_to(result[None], sums.shape)
    sigma[...] = extra[channels]


def combine_kernel(columns, place, sigma_at, sums, kept, taken, out):
    channels, frames = kept.shape[1:3]
    width = columns // BLOCKS
    halo = (LANES - width) // 2
    lane = lanes_of((1, LANES))
    total = jnp.sum(sums[...], axis=0)
    nu = [total] + [pltpu.roll(total, LANES - 8 * k, 1) for k in range(1, 6)]
    sigma = sigma_at[:1]
    g = [sigma * nu[k] - nu[k + 1] for k in range(5)]
    l1 = g[1] / g[0]
    l2 = g[2] / g[0]
    d1 = g[2] - l1 * g[1]
    e = g[3] - l1 * g[2]
    m = e / d1
    d2 = g[4] - l2 * g[2] - m * e
    z0 = nu[0]
    z1 = nu[1] - l1 * z0
    z2 = nu[2] - l2 * z0 - m * z1
    c2 = z2 / d2
    c1 = z1 / d1 - m * c2
    c0 = z0 / g[0] - l1 * c1 - l2 * c2

    tile_lane = lanes_of(TILE)
    tiles = -(-columns // LANES)
    odd = place[2] > 0.5
    for c in range(channels):
        w = [jnp.sum(jnp.where(lane == c, w, 0.0), axis=1, keepdims=True) for w in (c0, c1, c2)]
        for f in range(0, frames, 4):
            mine, other = [], []
            for i in range(f, f + 4):
                x = w[0] * kept[0, c, i] + w[1] * kept[1, c, i] + w[2] * kept[2, c, i]
                z = w[0] * taken[0, c, i] + w[1] * taken[1, c, i] + w[2] * taken[2, c, i]
                mine.append(jnp.where(odd, z, x))
                other.append(jnp.where(odd, x, z))
            turned = turn_pairs(mine) + turn_pairs(other)
            moved = [pltpu.roll(turned[s], (s * width - halo) % LANES, 1) for s in range(BLOCKS)]
            for t in range(tiles):
                piece = moved[t]
                if t + 1 < BLOCKS:
                    bound = width * (t + 1) - LANES * t
                    piece = jnp.where(tile_lane < bound, moved[t], moved[t + 1])
                count = min(LANES, columns - LANES * t)
                for i in range(4):
                    out[f + i, c, :, LANES * t : LANES * t + count] = piece[
                        2 * i : 2 * i + 2, :count
                    ]


def vmem():
    return pl.BlockSpec(memory_space=pltpu.VMEM)


def hbm():
    return pl.BlockSpec(memory_space=pltpu.HBM)


def params():
    return pltpu.CompilerParams(vmem_limit_bytes=32 << 20)


def shards(video, w_in, b_in, w_out, b_out, screen):
    count, me = lax.axis_size(AXIS), lax.axis_index(AXIS)
    _, channels, rows, columns = video.shape
    units = b_in.shape[0]
    frames = count
    across = -(-columns // LANES) * LANES
    operands = (w_in.T, b_in, w_out, b_out, screen, video)
    chunk = (channels, 2, 16, LANES)
    chunks, extra = pl.pallas_call(
        grade_kernel,
        out_shape=(
            jax.ShapeDtypeStruct((count,) + chunk, jnp.bfloat16),
            jax.ShapeDtypeStruct((channels + 1,) + TILE, jnp.float32),
        ),
        in_specs=[hbm()] * 6,
        out_specs=(hbm(),) * 2,
        scratch_shapes=[pltpu.SMEM(a.shape, a.dtype) for a in operands[:-1]]
        + [
            pltpu.VMEM(video.shape, video.dtype),
            pltpu.SemaphoreType.DMA((6,)),
            pltpu.SemaphoreType.DMA((channels + 1,)),
            pltpu.VMEM((channels, rows, across), jnp.float32),
            pltpu.VMEM((channels, 2, rows // 2) + TILE, jnp.float32),
            pltpu.VMEM((8 * units, LANES), jnp.float32),
            pltpu.VMEM((channels, units) + TILE, jnp.float32),
            pltpu.VMEM((channels, count) + chunk[1:], jnp.bfloat16),
            pltpu.VMEM((channels + 1,) + TILE, jnp.float32),
        ],
        name="grade",
    )(*operands)
    held = lax.all_to_all(chunks, AXIS, 0, 0)
    ends = [jnp.where(me // 2 == e, 1.0, 2.0) for e in (0, count // 2 - 1)]
    place = jnp.stack(ends + [jnp.where(me % 2 == 1, 1.0, 0.0)])
    place = jnp.broadcast_to(place[:, None, None], (3,) + TILE)
    fields = jax.ShapeDtypeStruct((3, channels, frames) + TILE, jnp.float32)
    sums, kept, given, sigma = pl.pallas_call(
        functools.partial(moment_kernel, columns),
        out_shape=(
            jax.ShapeDtypeStruct((count, 1, LANES), jnp.float32),
            fields,
            fields,
            jax.ShapeDtypeStruct(TILE, jnp.float32),
        ),
        in_specs=[vmem()] * 3,
        out_specs=(vmem(),) * 4,
        compiler_params=params(),
        name="moments",
    )(place, held, extra)
    taken = lax.ppermute(given, AXIS, [(i, i ^ 1) for i in range(count)])
    sums = lax.all_to_all(sums, AXIS, 0, 0)
    return pl.pallas_call(
        functools.partial(combine_kernel, columns),
        out_shape=jax.ShapeDtypeStruct((frames, channels, 2, columns), jnp.float32),
        in_specs=[vmem()] * 5,
        out_specs=vmem(),
        compiler_params=params(),
        name="combine",
    )(place, sigma, sums, kept, taken)


def solution(mesh):
    in_specs = (P(("video", AXIS), None, None, None), P(), P(), P(), P(), P())
    out_specs = P("video", None, AXIS, None)
    return jax.shard_map(shards, mesh=mesh, in_specs=in_specs, out_specs=out_specs, check_vma=False)
```

```python
import functools

import jax
import jax.numpy as jnp
from jax import lax
from jax.experimental import pallas as pl
from jax.experimental.pallas import tpu as pltpu
from jax.sharding import PartitionSpec as P

BLOCKS = 8
LANES = 128
TILE = (8, LANES)
AXIS = "tm"


def lanes_of(shape):
    return lax.broadcasted_iota(jnp.int32, shape, len(shape) - 1)


def sublanes_of(shape):
    return lax.broadcasted_iota(jnp.int32, shape, len(shape) - 2)


def first_member(count):
    return max(count * 3 // 4 - 1, 0)


def turn_pairs(tiles):
    sublane = sublanes_of(TILE)
    lower, even = sublane < 4, sublane % 4 < 2
    mixed = []
    for i in (0, 1):
        a, b = tiles[i], tiles[i + 2]
        mixed.append(
            (jnp.where(lower, a, pltpu.roll(b, 4, 0)), jnp.where(lower, pltpu.roll(a, 4, 0), b))
        )
    turned = []
    for i in (0, 1):
        a, b = mixed[0][i], mixed[1][i]
        turned.append(jnp.where(even, a, pltpu.roll(b, 2, 0)))
        turned.append(jnp.where(even, pltpu.roll(a, 6, 0), b))
    return turned


def three_parts(values, lane):
    high = values.astype(jnp.bfloat16).astype(jnp.float32)
    rest = values - high
    middle = rest.astype(jnp.bfloat16).astype(jnp.float32)
    third = LANES // 4
    return jnp.where(lane < third, high, jnp.where(lane < 2 * third, middle, rest - middle))


def grade_kernel(
    w_in_at, b_in_at, w_out_at, b_out_at, screen_at, video_at, chunks, extra,
    w_in, b_in, w_out, b_out, screen, video, arrived, sent,
    graded, tiles, first, second, ready, notes,
):
    channels, rows, columns = video.shape[1:]
    units = b_in.shape[0]
    across = graded.shape[2]
    width = columns // BLOCKS
    halo = (LANES - width) // 2
    chips = chunks.shape[0] // 2
    weights = [
        pltpu.make_async_copy(source, to, arrived.at[i])
        for i, (source, to) in enumerate(
            [
                (w_in_at, w_in), (b_in_at, b_in), (w_out_at, w_out),
                (b_out_at, b_out), (screen_at, screen),
            ]
        )
    ]
    pixels_in = pltpu.make_async_copy(video_at, video, arrived.at[5])
    pixels_in.start()
    for copy in weights:
        copy.start()
    for copy in weights:
        copy.wait()

    lane, sublane = lanes_of(TILE), sublanes_of(TILE)
    part = lane % (LANES // 4)
    used = lane < 3 * (LANES // 4)
    picks = [jnp.where(used & (part == 8 * c + sublane), 0.5, 0.0) for c in range(channels)]
    ones = jnp.where(used & (part == 8 * channels), 0.5, 0.0)
    mix = [[jnp.zeros(TILE, jnp.float32) for _ in range(channels + 1)] for _ in range(channels)]
    for j in range(units):
        into = [jnp.full(TILE, w_in[c, j]) for c in range(channels)] + [jnp.full(TILE, b_in[j])]
        values = ones * into[channels]
        for c in range(channels):
            values = values + picks[c] * into[c]
        first[8 * j : 8 * j + 8] = three_parts(values, lane)
        for c in range(channels):
            out = jnp.full(TILE, w_out[c, j])
            second[c, j] = out
            for k in range(channels + 1):
                mix[c][k] = mix[c][k] + (0.5 * out) * into[k]
    for c in range(channels):
        mix[c][c] = mix[c][c] + 1.0
        mix[c][channels] = mix[c][channels] + b_out[c]
    layer = first[...].astype(jnp.bfloat16)
    pixels_in.wait()

    span = across // 2
    times = span // LANES

    def wide(tile):
        return jnp.tile(tile, (1, times))

    def grade(step, _):
        top = pl.multiple_of(step * 16, 16)
        for start in range(0, across, span):
            count = min(span, columns - start)
            taken = []
            for c in range(channels):
                values = video[0, c, pl.ds(top, 16), start : start + count].astype(jnp.float32)
                if count < span:
                    empty = jnp.zeros((16, span - count), jnp.float32)
                    values = jnp.concatenate([values, empty], axis=1)
                taken.append(values)
            for r in (0, 8):
                pixels = [values[r : r + 8] for values in taken]
                group = jnp.concatenate(pixels + [jnp.ones((8, span), jnp.float32)], axis=0)
                group = group.astype(jnp.bfloat16)
                group = jnp.concatenate([group] * 3 + [jnp.zeros_like(group)], axis=0)
                half = jnp.dot(layer, group, preferred_element_type=jnp.float32)
                total = []
                for c in range(channels):
                    linear = wide(mix[c][channels])
                    for k in range(channels):
                        linear = linear + wide(mix[c][k]) * pixels[k]
                    total.append(linear)
                for j in range(units):
                    h = half[8 * j : 8 * j + 8]
                    unit = h * jnp.tanh(h)
                    for c in range(channels):
                        total[c] = total[c] + wide(second[c, j]) * unit
                inside = start + lanes_of((8, span)) < columns
                for c in range(channels):
                    graded[c, pl.ds(top + r, 8), start : start + span] = jnp.where(
                        inside, total[c], 0.0
                    )
        return 0

    lax.fori_loop(0, rows // 16, grade, 0)

    line = sublanes_of((rows, across))
    inside = lanes_of((rows, across)) < columns
    upper = sublane % 2 == 0
    zero = jnp.zeros(TILE, jnp.float32)
    sigma = jnp.full(TILE, 1.0, jnp.float32)
    copies = []
    for c in range(channels):
        sigma = jnp.where(lane == c, 6.0 + screen[c], sigma)
        g = graded[c]
        above = jnp.where(line == 0, 0.0, pltpu.roll(g, 1, 0))
        below = jnp.where(line == rows - 1, 0.0, pltpu.roll(g, rows - 1, 0))
        beside = pltpu.roll(g, 1, 1) + pltpu.roll(g, across - 1, 1)
        target = (screen[c] + 4.0) * g - (above + below + beside)
        target = jnp.where(inside, target, 0.0).astype(jnp.bfloat16).astype(jnp.float32)
        for top in range(0, rows, 8):
            band = target[top : top + 8]
            parts = []
            for s in range(BLOCKS):
                start = s * width - halo
                v, off = start // LANES, start % LANES
                low = zero
                if v >= 0:
                    low = pltpu.roll(band[:, v * LANES : (v + 1) * LANES], (LANES - off) % LANES, 1)
                high = pltpu.roll(band[:, (v + 1) * LANES : (v + 2) * LANES], LANES - off, 1)
                parts.append(jnp.where(lane < LANES - off, low, high))
            for side in range(2):
                for k, tile in enumerate(turn_pairs(parts[4 * side : 4 * side + 4])):
                    tiles[c, side, top // 2 + k] = tile
        pairs = rows // 2
        for side in range(2):

            def pair(k):
                return tiles[c, side, k] if 0 <= k < pairs else zero

            for q in range(chips):
                for p in range(2):
                    k = 2 * q - 1 + 2 * p
                    both = jnp.concatenate([pair(k), pair(k + 1)], axis=0)
                    at = (first_member(2 * chips) - (2 * q + side)) % (2 * chips)
                    ready[c, at, p] = both.astype(jnp.bfloat16)
        copies.append(pltpu.make_async_copy(ready.at[c], chunks.at[:, c], sent.at[c]))
        copies[-1].start()

    for c in range(channels):
        total = zero
        for side in range(2):
            field = [tiles[c, side, k] for k in range(pairs)]
            twice = []
            for k in range(pairs):
                beyond = zero
                if k > 0:
                    beyond = beyond + field[k - 1]
                if k < pairs - 1:
                    beyond = beyond + field[k + 1]
                own = 2.0 * field[k]
                if k == 0:
                    own = jnp.where(upper, field[k], own)
                if k == pairs - 1:
                    own = jnp.where(upper, own, field[k])
                twice.append(own + beyond)
            for k in range(pairs):
                after = pltpu.roll(twice[k + 1], 1, 0) if k < pairs - 1 else zero
                total = total + twice[k] * jnp.where(upper, pltpu.roll(twice[k], 7, 0), after)
        notes[c] = total + total
    notes[channels] = sigma
    copies.append(pltpu.make_async_copy(notes, extra, sent.at[channels]))
    copies[-1].start()
    for copy in copies:
        copy.wait()


def within(field, mask):
    zero = jnp.zeros_like(field[:1])
    frames = jnp.concatenate([field[1:], zero], axis=0) + jnp.concatenate([zero, field[:-1]], axis=0)
    beside = pltpu.roll(field, 1, 2) + pltpu.roll(field, LANES - 1, 2)
    return frames + jnp.where(mask, beside, 0.0)


def moment_kernel(columns, place, held, extra, sums, kept, given, sigma):
    frames, channels = held.shape[:2]
    width = columns // BLOCKS
    halo = (LANES - width) // 2
    odd = place[2] > 0.5
    lane, sublane = lanes_of(TILE), sublanes_of(TILE)
    block = sublane // 2 + jnp.where(odd, BLOCKS // 2, 0)
    column = block * width - halo + lane
    mask = ((column >= 0) & (column < columns))[None]
    own = (lane >= halo) & (lane < halo + width)
    upper = (sublane % 2 == 0)[None]
    top = jnp.where(upper, place[0][None], 2.0)
    bottom = jnp.where(upper, 2.0, place[1][None])
    out_lane = lanes_of((1, LANES))
    result = jnp.zeros((1, LANES), jnp.float32)
    for c in range(channels):
        turn = first_member(frames) + 1
        halves = [
            jnp.concatenate([held[turn:, c, p], held[:turn, c, p]], axis=0).astype(jnp.float32)
            for p in range(2)
        ]
        b = [halves[0][:, :8], halves[0][:, 8:], halves[1][:, :8], halves[1][:, 8:]]
        between = [b[i] + b[i + 1] for i in range(3)]
        totals = [jnp.zeros(TILE, jnp.float32) for _ in range(6)]
        totals[5] = extra[c]
        sides = []
        for i in (1, 2):
            u0 = b[i]
            u1 = jnp.where(upper, pltpu.roll(between[i - 1], 7, 1), pltpu.roll(between[i], 1, 1))
            u2 = b[i - 1] + (top if i == 1 else bottom) * u0 + b[i + 1]
            k0 = within(u0, mask)
            k1 = within(u1, mask)
            y = 2.0 * k1 + within(k0, mask)
            y1 = 2.0 * within(u2, mask) + within(k1, mask)
            n1 = u1 + k0
            n2 = u2 + y
            sides.append((u0, n1, n2))
            products = [
                u0 * u0,
                u0 * n1,
                n1 * n1,
                n1 * n2,
                n2 * n2,
                n2 * within(n2, mask) + y * y1 + 2.0 * (y1 * u2),
            ]
            for k, product in enumerate(products):
                totals[k] = totals[k] + jnp.sum(product, axis=0)
        for k in range(3):
            kept[k, c] = jnp.where(odd[None], sides[1][k], sides[0][k])
            given[k, c] = jnp.where(odd[None], sides[0][k], sides[1][k])
        for k, total in enumerate(totals):
            total = jnp.where(own, total, 0.0)
            total = jnp.sum(total, axis=0, keepdims=True)
            total = jnp.sum(total, axis=1, keepdims=True)
            result = jnp.where(out_lane == 8 * k + c, total, result)
    sums[...] = jnp.broadcast_to(result[None], sums.shape)
    sigma[...] = extra[channels]


def combine_kernel(columns, place, sigma_at, sums, kept, taken, out):
    channels, frames = kept.shape[1:3]
    width = columns // BLOCKS
    halo = (LANES - width) // 2
    lane = lanes_of((1, LANES))
    total = jnp.sum(sums[...], axis=0)
    nu = [total] + [pltpu.roll(total, LANES - 8 * k, 1) for k in range(1, 6)]
    sigma = sigma_at[:1]
    g = [sigma * nu[k] - nu[k + 1] for k in range(5)]
    l1 = g[1] / g[0]
    l2 = g[2] / g[0]
    d1 = g[2] - l1 * g[1]
    e = g[3] - l1 * g[2]
    m = e / d1
    d2 = g[4] - l2 * g[2] - m * e
    z0 = nu[0]
    z1 = nu[1] - l1 * z0
    z2 = nu[2] - l2 * z0 - m * z1
    c2 = z2 / d2
    c1 = z1 / d1 - m * c2
    c0 = z0 / g[0] - l1 * c1 - l2 * c2

    tile_lane = lanes_of(TILE)
    tiles = -(-columns // LANES)
    odd = place[2] > 0.5
    for c in range(channels):
        w = [jnp.sum(jnp.where(lane == c, w, 0.0), axis=1, keepdims=True) for w in (c0, c1, c2)]
        for f in range(0, frames, 4):
            mine, other = [], []
            for i in range(f, f + 4):
                x = w[0] * kept[0, c, i] + w[1] * kept[1, c, i] + w[2] * kept[2, c, i]
                z = w[0] * taken[0, c, i] + w[1] * taken[1, c, i] + w[2] * taken[2, c, i]
                mine.append(jnp.where(odd, z, x))
                other.append(jnp.where(odd, x, z))
            turned = turn_pairs(mine) + turn_pairs(other)
            moved = [pltpu.roll(turned[s], (s * width - halo) % LANES, 1) for s in range(BLOCKS)]
            for t in range(tiles):
                piece = moved[t]
                if t + 1 < BLOCKS:
                    bound = width * (t + 1) - LANES * t
                    piece = jnp.where(tile_lane < bound, moved[t], moved[t + 1])
                count = min(LANES, columns - LANES * t)
                for i in range(4):
                    out[frames - 1 - (f + i), c, :, LANES * t : LANES * t + count] = piece[
                        2 * i : 2 * i + 2, :count
                    ]


def vmem():
    return pl.BlockSpec(memory_space=pltpu.VMEM)


def hbm():
    return pl.BlockSpec(memory_space=pltpu.HBM)


def params():
    return pltpu.CompilerParams(vmem_limit_bytes=32 << 20)


def shards(video, w_in, b_in, w_out, b_out, screen):
    count, me = lax.axis_size(AXIS), lax.axis_index(AXIS)
    _, channels, rows, columns = video.shape
    units = b_in.shape[0]
    frames = count
    across = -(-columns // LANES) * LANES
    operands = (w_in.T, b_in, w_out, b_out, screen, video)
    chunk = (channels, 2, 16, LANES)
    chunks, extra = pl.pallas_call(
        grade_kernel,
        out_shape=(
            jax.ShapeDtypeStruct((count,) + chunk, jnp.bfloat16),
            jax.ShapeDtypeStruct((channels + 1,) + TILE, jnp.float32),
        ),
        in_specs=[hbm()] * 6,
        out_specs=(hbm(),) * 2,
        scratch_shapes=[pltpu.SMEM(a.shape, a.dtype) for a in operands[:-1]]
        + [
            pltpu.VMEM(video.shape, video.dtype),
            pltpu.SemaphoreType.DMA((6,)),
            pltpu.SemaphoreType.DMA((channels + 1,)),
            pltpu.VMEM((channels, rows, across), jnp.float32),
            pltpu.VMEM((channels, 2, rows // 2) + TILE, jnp.float32),
            pltpu.VMEM((8 * units, LANES), jnp.float32),
            pltpu.VMEM((channels, units) + TILE, jnp.float32),
            pltpu.VMEM((channels, count) + chunk[1:], jnp.bfloat16),
            pltpu.VMEM((channels + 1,) + TILE, jnp.float32),
        ],
        name="grade",
    )(*operands)
    first = first_member(count)
    order = [(first - i) % count for i in range(count)]
    held = lax.all_to_all(chunks, AXIS, 0, 0, axis_index_groups=[order])
    ends = [jnp.where(me // 2 == e, 1.0, 2.0) for e in (0, count // 2 - 1)]
    place = jnp.stack(ends + [jnp.where(me % 2 == 1, 1.0, 0.0)])
    place = jnp.broadcast_to(place[:, None, None], (3,) + TILE)
    fields = jax.ShapeDtypeStruct((3, channels, frames) + TILE, jnp.float32)
    sums, kept, given, sigma = pl.pallas_call(
        functools.partial(moment_kernel, columns),
        out_shape=(
            jax.ShapeDtypeStruct((count, 1, LANES), jnp.float32),
            fields,
            fields,
            jax.ShapeDtypeStruct(TILE, jnp.float32),
        ),
        in_specs=[vmem()] * 3,
        out_specs=(vmem(),) * 4,
        compiler_params=params(),
        name="moments",
    )(place, held, extra)
    taken = lax.ppermute(given, AXIS, [(i, i ^ 1) for i in range(count)])
    down = list(range(count))[::-1]
    sums = lax.all_to_all(sums, AXIS, 0, 0, axis_index_groups=[down])
    return pl.pallas_call(
        functools.partial(combine_kernel, columns),
        out_shape=jax.ShapeDtypeStruct((frames, channels, 2, columns), jnp.float32),
        in_specs=[vmem()] * 5,
        out_specs=vmem(),
        compiler_params=params(),
        name="combine",
    )(place, sigma, sums, kept, taken)


def solution(mesh):
    in_specs = (P(("video", AXIS), None, None, None), P(), P(), P(), P(), P())
    out_specs = P("video", None, AXIS, None)
    return jax.shard_map(shards, mesh=mesh, in_specs=in_specs, out_specs=out_specs, check_vma=False)
```

```python
import functools

import jax
import jax.numpy as jnp
from jax import lax
from jax.experimental import pallas as pl
from jax.experimental.pallas import tpu as pltpu
from jax.sharding import PartitionSpec as P

BLOCKS = 8
LANES = 128
TILE = (8, LANES)
AXIS = "tm"


def lanes_of(shape):
    return lax.broadcasted_iota(jnp.int32, shape, len(shape) - 1)


def sublanes_of(shape):
    return lax.broadcasted_iota(jnp.int32, shape, len(shape) - 2)


def first_member(count):
    return max(count * 3 // 4 - 1, 0)


def turn_pairs(tiles):
    sublane = sublanes_of(TILE)
    lower, even = sublane < 4, sublane % 4 < 2
    mixed = []
    for i in (0, 1):
        a, b = tiles[i], tiles[i + 2]
        mixed.append(
            (jnp.where(lower, a, pltpu.roll(b, 4, 0)), jnp.where(lower, pltpu.roll(a, 4, 0), b))
        )
    turned = []
    for i in (0, 1):
        a, b = mixed[0][i], mixed[1][i]
        turned.append(jnp.where(even, a, pltpu.roll(b, 2, 0)))
        turned.append(jnp.where(even, pltpu.roll(a, 6, 0), b))
    return turned


def three_parts(values, lane):
    high = values.astype(jnp.bfloat16).astype(jnp.float32)
    rest = values - high
    middle = rest.astype(jnp.bfloat16).astype(jnp.float32)
    third = LANES // 4
    return jnp.where(lane < third, high, jnp.where(lane < 2 * third, middle, rest - middle))


def grade_kernel(
    w_in_at, b_in_at, w_out_at, b_out_at, screen_at, video_at, chunks,
    w_in, b_in, w_out, b_out, screen, video, arrived, sent, graded, first, second, ready,
):
    channels, rows, columns = video.shape[1:]
    units = b_in.shape[0]
    across = -(-columns // LANES) * LANES
    width = columns // BLOCKS
    halo = (LANES - width) // 2
    chips = chunks.shape[0] // 2
    weights = [
        pltpu.make_async_copy(source, to, arrived.at[i])
        for i, (source, to) in enumerate(
            [
                (w_in_at, w_in), (b_in_at, b_in), (w_out_at, w_out),
                (b_out_at, b_out), (screen_at, screen),
            ]
        )
    ]

    def pixels_in(step):
        part = (slice(None), slice(None), pl.ds(pl.multiple_of(step * 16, 16), 16))
        return pltpu.make_async_copy(video_at.at[part], video.at[part], arrived.at[5 + step])

    for step in range(rows // 16):
        pixels_in(step).start()
    for copy in weights:
        copy.start()
    for copy in weights:
        copy.wait()

    lane, sublane = lanes_of(TILE), sublanes_of(TILE)
    part = lane % (LANES // 4)
    used = lane < 3 * (LANES // 4)
    picks = [jnp.where(used & (part == 8 * c + sublane), 0.5, 0.0) for c in range(channels)]
    ones = jnp.where(used & (part == 8 * channels), 0.5, 0.0)
    mix = [[jnp.zeros(TILE, jnp.float32) for _ in range(channels + 1)] for _ in range(channels)]
    for j in range(units):
        into = [jnp.full(TILE, w_in[c, j]) for c in range(channels)] + [jnp.full(TILE, b_in[j])]
        values = ones * into[channels]
        for c in range(channels):
            values = values + picks[c] * into[c]
        first[8 * j : 8 * j + 8] = three_parts(values, lane)
        for c in range(channels):
            out = jnp.full(TILE, w_out[c, j])
            second[c, j] = out
            for k in range(channels + 1):
                mix[c][k] = mix[c][k] + (0.5 * out) * into[k]
    for c in range(channels):
        mix[c][c] = mix[c][c] + 1.0
        mix[c][channels] = mix[c][channels] + b_out[c]
    layer = first[...].astype(jnp.bfloat16)

    half_blocks = BLOCKS // 2
    span = half_blocks * LANES
    zero = jnp.zeros(TILE, jnp.float32)
    upper = sublane % 2 == 0
    masks = []
    for side in range(2):
        column = (sublane // 2 + side * half_blocks) * width - halo + lane
        masks.append((column >= 0) & (column < columns))

    def wide(tile):
        return jnp.tile(tile, (1, half_blocks))

    def cut(band):
        parts = []
        for s in range(BLOCKS):
            start = s * width - halo
            v, off = start // LANES, start % LANES
            low = band[:, v * LANES : (v + 1) * LANES] if v >= 0 else zero
            high = band[:, (v + 1) * LANES : (v + 2) * LANES]
            parts.append(pltpu.roll(jnp.where(lane >= off, low, high), LANES - off, 1))
        return turn_pairs(parts[:half_blocks]), turn_pairs(parts[half_blocks:])

    def grade(step, _):
        pixels_in(step).wait()
        top = pl.multiple_of(step * 16, 16)
        taken = []
        for c in range(channels):
            values = video[0, c, pl.ds(top, 16), :].astype(jnp.float32)
            empty = jnp.zeros((16, across - columns), jnp.float32)
            taken.append(jnp.concatenate([values, empty], axis=1))
        for r in (0, 8):
            sides = [cut(values[r : r + 8]) for values in taken]
            for side in range(2):
                pixels = [jnp.concatenate(sides[c][side], axis=1) for c in range(channels)]
                group = jnp.concatenate(pixels + [jnp.ones((8, span), jnp.float32)], axis=0)
                group = group.astype(jnp.bfloat16)
                group = jnp.concatenate([group] * 3 + [jnp.zeros_like(group)], axis=0)
                half = jnp.dot(layer, group, preferred_element_type=jnp.float32)
                total = []
                for c in range(channels):
                    linear = wide(mix[c][channels])
                    for k in range(channels):
                        linear = linear + wide(mix[c][k]) * pixels[k]
                    total.append(linear)
                for j in range(units):
                    h = half[8 * j : 8 * j + 8]
                    unit = h * jnp.tanh(h)
                    for c in range(channels):
                        total[c] = total[c] + wide(second[c, j]) * unit
                for c in range(channels):
                    for k in range(half_blocks):
                        tile = total[c][:, k * LANES : (k + 1) * LANES]
                        at = step * 8 + r // 2 + k
                        graded[c, side, at] = jnp.where(masks[side], tile, 0.0)
        return 0

    lax.fori_loop(0, rows // 16, grade, 0, unroll=2)

    pairs = rows // 2
    copies = []
    for c in range(channels):
        for side in range(2):
            field = [graded[c, side, k] for k in range(pairs)]
            between = [
                field[0], *[field[k] + field[k + 1] for k in range(pairs - 1)], field[pairs - 1]
            ]
            target = [zero]
            for k in range(pairs):
                beyond = jnp.where(
                    upper, pltpu.roll(between[k], 7, 0), pltpu.roll(between[k + 1], 1, 0)
                )
                beyond = beyond + (pltpu.roll(field[k], 1, 1) + pltpu.roll(field[k], LANES - 1, 1))
                value = (screen[c] + 4.0) * field[k] - beyond
                target.append(jnp.where(masks[side], value, 0.0))
            target.append(zero)
            for q in range(chips):
                at = (first_member(2 * chips) - (2 * q + side)) % (2 * chips)
                for p in range(2):
                    k = 2 * q + 2 * p
                    both = jnp.concatenate([target[k], target[k + 1]], axis=0)
                    ready[c, at, p] = both.astype(jnp.bfloat16)
        copies.append(pltpu.make_async_copy(ready.at[c], chunks.at[:, c], sent.at[c]))
        copies[-1].start()
    for copy in copies:
        copy.wait()


def fifth_kernel(screen, chunks, extra):
    chips, channels = chunks.shape[0] // 2, chunks.shape[1]
    upper = sublanes_of(TILE) % 2 == 0
    zero = jnp.zeros(TILE, jnp.float32)
    sigma = jnp.full(TILE, 1.0, jnp.float32)
    pairs = 2 * chips
    for c in range(channels):
        sigma = jnp.where(lanes_of(TILE) == c, 6.0 + screen[c], sigma)
        total = zero
        for side in range(2):
            field = []
            for q in range(chips):
                at = (first_member(2 * chips) - (2 * q + side)) % (2 * chips)
                field.append(chunks[at, c, 0].astype(jnp.float32)[8:])
                field.append(chunks[at, c, 1].astype(jnp.float32)[:8])
            twice = []
            for k in range(pairs):
                beyond = zero
                if k > 0:
                    beyond = beyond + field[k - 1]
                if k < pairs - 1:
                    beyond = beyond + field[k + 1]
                own = 2.0 * field[k]
                if k == 0:
                    own = jnp.where(upper, field[k], own)
                if k == pairs - 1:
                    own = jnp.where(upper, own, field[k])
                twice.append(own + beyond)
            for k in range(pairs):
                after = pltpu.roll(twice[k + 1], 1, 0) if k < pairs - 1 else zero
                total = total + twice[k] * jnp.where(upper, pltpu.roll(twice[k], 7, 0), after)
        extra[c] = total + total
    extra[channels] = sigma


def within(field, mask):
    zero = jnp.zeros_like(field[:1])
    frames = jnp.concatenate([field[1:], zero], axis=0) + jnp.concatenate([zero, field[:-1]], axis=0)
    beside = pltpu.roll(field, 1, 2) + pltpu.roll(field, LANES - 1, 2)
    return frames + jnp.where(mask, beside, 0.0)


def half_form(field):
    zero = jnp.zeros_like(field[:1])
    return field * (jnp.concatenate([zero, field[:-1]], axis=0) + pltpu.roll(field, 1, 2))


GAMMA = (5.0 - 5.0**0.5) / 4.0
DELTA = (5.0 + 5.0**0.5) / 10.0


def moment_kernel(columns, place, held, extra, sums, kept, given, sigma):
    frames, channels = held.shape[:2]
    width = columns // BLOCKS
    halo = (LANES - width) // 2
    odd = place[2] > 0.5
    lane, sublane = lanes_of(TILE), sublanes_of(TILE)
    block = sublane // 2 + jnp.where(odd, BLOCKS // 2, 0)
    column = block * width - halo + lane
    mask = ((column >= 0) & (column < columns))[None]
    own = (lane >= halo) & (lane < halo + width)
    upper = (sublane % 2 == 0)[None]
    top = jnp.where(upper, place[0][None], 2.0)
    bottom = jnp.where(upper, 2.0, place[1][None])
    out_lane = lanes_of((1, LANES))
    result = jnp.zeros((1, LANES), jnp.float32)
    for c in range(channels):
        turn = first_member(frames) + 1
        halves = [
            jnp.concatenate([held[turn:, c, p], held[:turn, c, p]], axis=0).astype(jnp.float32)
            for p in range(2)
        ]
        b = [halves[0][:, :8], halves[0][:, 8:], halves[1][:, :8], halves[1][:, 8:]]
        between = [b[i] + b[i + 1] for i in range(3)]
        totals = [jnp.zeros(TILE, jnp.float32) for _ in range(6)]
        totals[5] = extra[c]
        sides = []
        for i in (1, 2):
            u0 = b[i]
            u1 = jnp.where(upper, pltpu.roll(between[i - 1], 7, 1), pltpu.roll(between[i], 1, 1))
            u2 = b[i - 1] + (top if i == 1 else bottom) * u0 + b[i + 1]
            k0 = within(u0, mask)
            k1 = within(u1, mask)
            kk0 = within(k0, mask)
            n1 = u1 + k0
            n2 = u2 + 2.0 * k1 + kk0
            z = kk0 + 2.5 * k1 + GAMMA * u2
            t = u2 + DELTA * k1
            sides.append((u0, n1, n2))
            products = [
                u0 * u0,
                u0 * n1,
                n1 * n1,
                n1 * n2,
                n2 * n2,
                2.0 * half_form(z) + (2.0 * (5.0 - GAMMA * GAMMA)) * half_form(t),
            ]
            for k, product in enumerate(products):
                totals[k] = totals[k] + jnp.sum(product, axis=0)
        for k in range(3):
            kept[k, c] = jnp.where(odd[None], sides[1][k], sides[0][k])
            given[k, c] = jnp.where(odd[None], sides[0][k], sides[1][k])
        for k, total in enumerate(totals):
            total = jnp.where(own, total, 0.0)
            total = jnp.sum(total, axis=0, keepdims=True)
            total = jnp.sum(total, axis=1, keepdims=True)
            result = jnp.where(out_lane == 8 * k + c, total, result)
    sums[...] = jnp.broadcast_to(result[None], sums.shape)
    sigma[...] = extra[channels]


def combine_kernel(columns, place, sigma_at, sums, kept, taken, out):
    channels, frames = kept.shape[1:3]
    width = columns // BLOCKS
    halo = (LANES - width) // 2
    lane = lanes_of((1, LANES))
    total = jnp.sum(sums[...], axis=0)
    nu = [total] + [pltpu.roll(total, LANES - 8 * k, 1) for k in range(1, 6)]
    sigma = sigma_at[:1]
    g = [sigma * nu[k] - nu[k + 1] for k in range(5)]
    l1 = g[1] / g[0]
    l2 = g[2] / g[0]
    d1 = g[2] - l1 * g[1]
    e = g[3] - l1 * g[2]
    m = e / d1
    d2 = g[4] - l2 * g[2] - m * e
    z0 = nu[0]
    z1 = nu[1] - l1 * z0
    z2 = nu[2] - l2 * z0 - m * z1
    c2 = z2 / d2
    c1 = z1 / d1 - m * c2
    c0 = z0 / g[0] - l1 * c1 - l2 * c2

    tile_lane = lanes_of(TILE)
    tiles = -(-columns // LANES)
    odd = place[2] > 0.5
    for c in range(channels):
        w = [jnp.sum(jnp.where(lane == c, w, 0.0), axis=1, keepdims=True) for w in (c0, c1, c2)]
        for f in range(0, frames, 4):
            mine, other = [], []
            for i in range(f, f + 4):
                x = w[0] * kept[0, c, i] + w[1] * kept[1, c, i] + w[2] * kept[2, c, i]
                z = w[0] * taken[0, c, i] + w[1] * taken[1, c, i] + w[2] * taken[2, c, i]
                mine.append(jnp.where(odd, z, x))
                other.append(jnp.where(odd, x, z))
            turned = turn_pairs(mine) + turn_pairs(other)
            moved = [pltpu.roll(turned[s], (s * width - halo) % LANES, 1) for s in range(BLOCKS)]
            for t in range(tiles):
                piece = moved[t]
                if t + 1 < BLOCKS:
                    bound = width * (t + 1) - LANES * t
                    piece = jnp.where(tile_lane < bound, moved[t], moved[t + 1])
                count = min(LANES, columns - LANES * t)
                for i in range(4):
                    out[frames - 1 - (f + i), c, :, LANES * t : LANES * t + count] = piece[
                        2 * i : 2 * i + 2, :count
                    ]


def vmem():
    return pl.BlockSpec(memory_space=pltpu.VMEM)


def hbm():
    return pl.BlockSpec(memory_space=pltpu.HBM)


def params():
    return pltpu.CompilerParams(vmem_limit_bytes=32 << 20)


def shards(video, w_in, b_in, w_out, b_out, screen):
    count, me = lax.axis_size(AXIS), lax.axis_index(AXIS)
    _, channels, rows, columns = video.shape
    units = b_in.shape[0]
    frames = count
    operands = (w_in.T, b_in, w_out, b_out, screen, video)
    chunk = (channels, 2, 16, LANES)
    chunks = pl.pallas_call(
        grade_kernel,
        out_shape=jax.ShapeDtypeStruct((count,) + chunk, jnp.bfloat16),
        in_specs=[hbm()] * 6,
        out_specs=hbm(),
        scratch_shapes=[pltpu.SMEM(a.shape, a.dtype) for a in operands[:-1]]
        + [
            pltpu.VMEM(video.shape, video.dtype),
            pltpu.SemaphoreType.DMA((5 + rows // 16,)),
            pltpu.SemaphoreType.DMA((channels,)),
            pltpu.VMEM((channels, 2, rows // 2) + TILE, jnp.float32),
            pltpu.VMEM((8 * units, LANES), jnp.float32),
            pltpu.VMEM((channels, units) + TILE, jnp.float32),
            pltpu.VMEM((channels, count) + chunk[1:], jnp.bfloat16),
        ],
        name="grade",
    )(*operands)
    extra = pl.pallas_call(
        fifth_kernel,
        out_shape=jax.ShapeDtypeStruct((channels + 1,) + TILE, jnp.float32),
        in_specs=[pl.BlockSpec(memory_space=pltpu.SMEM), vmem()],
        out_specs=vmem(),
        compiler_params=params(),
        cost_estimate=pl.CostEstimate(flops=1 << 20, bytes_accessed=1 << 20, transcendentals=0),
        name="fifth",
    )(screen, chunks)
    first = first_member(count)
    order = [(first - i) % count for i in range(count)]
    held = lax.all_to_all(chunks, AXIS, 0, 0, axis_index_groups=[order])
    ends = [jnp.where(me // 2 == e, 1.0, 2.0) for e in (0, count // 2 - 1)]
    place = jnp.stack(ends + [jnp.where(me % 2 == 1, 1.0, 0.0)])
    place = jnp.broadcast_to(place[:, None, None], (3,) + TILE)
    fields = jax.ShapeDtypeStruct((3, channels, frames) + TILE, jnp.float32)
    sums, kept, given, sigma = pl.pallas_call(
        functools.partial(moment_kernel, columns),
        out_shape=(
            jax.ShapeDtypeStruct((count, 1, LANES), jnp.float32),
            fields,
            fields,
            jax.ShapeDtypeStruct(TILE, jnp.float32),
        ),
        in_specs=[vmem()] * 3,
        out_specs=(vmem(),) * 4,
        compiler_params=params(),
        name="moments",
    )(place, held, extra)
    taken = lax.ppermute(given, AXIS, [(i, i ^ 1) for i in range(count)])
    down = list(range(count))[::-1]
    sums = lax.all_to_all(sums, AXIS, 0, 0, axis_index_groups=[down])
    return pl.pallas_call(
        functools.partial(combine_kernel, columns),
        out_shape=jax.ShapeDtypeStruct((frames, channels, 2, columns), jnp.float32),
        in_specs=[vmem()] * 5,
        out_specs=vmem(),
        compiler_params=params(),
        name="combine",
    )(place, sigma, sums, kept, taken)


def solution(mesh):
    in_specs = (P(("video", AXIS), None, None, None), P(), P(), P(), P(), P())
    out_specs = P("video", None, AXIS, None)
    return jax.shard_map(shards, mesh=mesh, in_specs=in_specs, out_specs=out_specs, check_vma=False)
```

```python
import functools

import jax
import jax.numpy as jnp
from jax import lax
from jax.experimental import pallas as pl
from jax.experimental.pallas import tpu as pltpu
from jax.sharding import PartitionSpec as P

BLOCKS = 8
LANES = 128
TILE = (8, LANES)
AXIS = "tm"


def lanes_of(shape):
    return lax.broadcasted_iota(jnp.int32, shape, len(shape) - 1)


def sublanes_of(shape):
    return lax.broadcasted_iota(jnp.int32, shape, len(shape) - 2)


def first_member(count):
    return max(count * 3 // 4 - 1, 0)


def turn_pairs(tiles):
    sublane = sublanes_of(TILE)
    lower, even = sublane < 4, sublane % 4 < 2
    mixed = []
    for i in (0, 1):
        a, b = tiles[i], tiles[i + 2]
        mixed.append(
            (jnp.where(lower, a, pltpu.roll(b, 4, 0)), jnp.where(lower, pltpu.roll(a, 4, 0), b))
        )
    turned = []
    for i in (0, 1):
        a, b = mixed[0][i], mixed[1][i]
        turned.append(jnp.where(even, a, pltpu.roll(b, 2, 0)))
        turned.append(jnp.where(even, pltpu.roll(a, 6, 0), b))
    return turned


def three_parts(values, lane):
    high = values.astype(jnp.bfloat16).astype(jnp.float32)
    rest = values - high
    middle = rest.astype(jnp.bfloat16).astype(jnp.float32)
    third = LANES // 4
    return jnp.where(lane < third, high, jnp.where(lane < 2 * third, middle, rest - middle))


def grade_kernel(
    w_in_at, b_in_at, w_out_at, b_out_at, screen_at, video_at, chunks,
    w_in, b_in, w_out, b_out, screen, video, arrived, sent, graded, first, second, ready,
):
    channels, rows, columns = video.shape[1:]
    units = b_in.shape[0]
    across = -(-columns // LANES) * LANES
    width = columns // BLOCKS
    halo = (LANES - width) // 2
    chips = chunks.shape[0] // 2
    weights = [
        pltpu.make_async_copy(source, to, arrived.at[i])
        for i, (source, to) in enumerate(
            [
                (w_in_at, w_in), (b_in_at, b_in), (w_out_at, w_out),
                (b_out_at, b_out), (screen_at, screen),
            ]
        )
    ]

    def pixels_in(step):
        part = (slice(None), slice(None), pl.ds(pl.multiple_of(step * 16, 16), 16))
        return pltpu.make_async_copy(video_at.at[part], video.at[part], arrived.at[5 + step])

    for step in range(rows // 16):
        pixels_in(step).start()
    for copy in weights:
        copy.start()
    for copy in weights:
        copy.wait()

    lane, sublane = lanes_of(TILE), sublanes_of(TILE)
    part = lane % (LANES // 4)
    used = lane < 3 * (LANES // 4)
    picks = [jnp.where(used & (part == 8 * c + sublane), 0.5, 0.0) for c in range(channels)]
    ones = jnp.where(used & (part == 8 * channels), 0.5, 0.0)
    mix = [[jnp.zeros(TILE, jnp.float32) for _ in range(channels + 1)] for _ in range(channels)]
    for j in range(units):
        into = [jnp.full(TILE, w_in[c, j]) for c in range(channels)] + [jnp.full(TILE, b_in[j])]
        values = ones * into[channels]
        for c in range(channels):
            values = values + picks[c] * into[c]
        first[8 * j : 8 * j + 8] = three_parts(values, lane)
        for c in range(channels):
            out = jnp.full(TILE, w_out[c, j])
            second[c, j] = out
            for k in range(channels + 1):
                mix[c][k] = mix[c][k] + (0.5 * out) * into[k]
    for c in range(channels):
        mix[c][c] = mix[c][c] + 1.0
        mix[c][channels] = mix[c][channels] + b_out[c]
    layer = first[...].astype(jnp.bfloat16)

    half_blocks = BLOCKS // 2
    span = half_blocks * LANES
    zero = jnp.zeros(TILE, jnp.float32)
    upper = sublane % 2 == 0
    masks = []
    for side in range(2):
        column = (sublane // 2 + side * half_blocks) * width - halo + lane
        masks.append((column >= 0) & (column < columns))

    def wide(tile):
        return jnp.tile(tile, (1, half_blocks))

    def cut(band):
        parts = []
        for s in range(BLOCKS):
            start = s * width - halo
            v, off = start // LANES, start % LANES
            low = band[:, v * LANES : (v + 1) * LANES] if v >= 0 else zero
            high = band[:, (v + 1) * LANES : (v + 2) * LANES]
            parts.append(pltpu.roll(jnp.where(lane >= off, low, high), LANES - off, 1))
        return turn_pairs(parts[:half_blocks]), turn_pairs(parts[half_blocks:])

    def grade(step, _):
        pixels_in(step).wait()
        top = pl.multiple_of(step * 16, 16)
        taken = []
        for c in range(channels):
            values = video[0, c, pl.ds(top, 16), :].astype(jnp.float32)
            empty = jnp.zeros((16, across - columns), jnp.float32)
            taken.append(jnp.concatenate([values, empty], axis=1))
        for r in (0, 8):
            sides = [cut(values[r : r + 8]) for values in taken]
            for side in range(2):
                pixels = [jnp.concatenate(sides[c][side], axis=1) for c in range(channels)]
                group = jnp.concatenate(pixels + [jnp.ones((8, span), jnp.float32)], axis=0)
                group = group.astype(jnp.bfloat16)
                group = jnp.concatenate([group] * 3 + [jnp.zeros_like(group)], axis=0)
                half = jnp.dot(layer, group, preferred_element_type=jnp.float32)
                total = []
                for c in range(channels):
                    linear = wide(mix[c][channels])
                    for k in range(channels):
                        linear = linear + wide(mix[c][k]) * pixels[k]
                    total.append(linear)
                for j in range(units):
                    h = half[8 * j : 8 * j + 8]
                    unit = h * jnp.tanh(h)
                    for c in range(channels):
                        total[c] = total[c] + wide(second[c, j]) * unit
                for c in range(channels):
                    for k in range(half_blocks):
                        tile = total[c][:, k * LANES : (k + 1) * LANES]
                        at = step * 8 + r // 2 + k
                        graded[c, side, at] = jnp.where(masks[side], tile, 0.0)
        return 0

    lax.fori_loop(0, rows // 16, grade, 0, unroll=2)

    pairs = rows // 2
    copies = []
    for c in range(channels):
        for side in range(2):
            field = [graded[c, side, k] for k in range(pairs)]
            between = [
                field[0], *[field[k] + field[k + 1] for k in range(pairs - 1)], field[pairs - 1]
            ]
            target = [zero]
            for k in range(pairs):
                beyond = jnp.where(
                    upper, pltpu.roll(between[k], 7, 0), pltpu.roll(between[k + 1], 1, 0)
                )
                beyond = beyond + (pltpu.roll(field[k], 1, 1) + pltpu.roll(field[k], LANES - 1, 1))
                value = (screen[c] + 4.0) * field[k] - beyond
                target.append(jnp.where(masks[side], value, 0.0))
            target.append(zero)
            for q in range(chips):
                at = (first_member(2 * chips) - (2 * q + side)) % (2 * chips)
                for p in range(2):
                    k = 2 * q + 2 * p
                    both = jnp.concatenate([target[k], target[k + 1]], axis=0)
                    ready[c, at, p] = both.astype(jnp.bfloat16)
        copies.append(pltpu.make_async_copy(ready.at[c], chunks.at[:, c], sent.at[c]))
        copies[-1].start()
    for copy in copies:
        copy.wait()


def fifth_kernel(screen, chunks, extra):
    chips, channels = chunks.shape[0] // 2, chunks.shape[1]
    upper = sublanes_of(TILE) % 2 == 0
    zero = jnp.zeros(TILE, jnp.float32)
    sigma = jnp.full(TILE, 1.0, jnp.float32)
    pairs = 2 * chips
    for c in range(channels):
        sigma = jnp.where(lanes_of(TILE) == c, 6.0 + screen[c], sigma)
        total = zero
        for side in range(2):
            field = []
            for q in range(chips):
                at = (first_member(2 * chips) - (2 * q + side)) % (2 * chips)
                field.append(chunks[at, c, 0].astype(jnp.float32)[8:])
                field.append(chunks[at, c, 1].astype(jnp.float32)[:8])
            twice = []
            for k in range(pairs):
                beyond = zero
                if k > 0:
                    beyond = beyond + field[k - 1]
                if k < pairs - 1:
                    beyond = beyond + field[k + 1]
                own = 2.0 * field[k]
                if k == 0:
                    own = jnp.where(upper, field[k], own)
                if k == pairs - 1:
                    own = jnp.where(upper, own, field[k])
                twice.append(own + beyond)
            for k in range(pairs):
                after = pltpu.roll(twice[k + 1], 1, 0) if k < pairs - 1 else zero
                total = total + twice[k] * jnp.where(upper, pltpu.roll(twice[k], 7, 0), after)
        extra[c] = total + total
    extra[channels] = sigma


def frames_of(field):
    zero = jnp.zeros_like(field[:1])
    return jnp.concatenate([field[1:], zero], axis=0) + jnp.concatenate([zero, field[:-1]], axis=0)


def rows_of(before, after):
    upper = (sublanes_of(TILE) % 2 == 0)[None]
    return jnp.where(upper, pltpu.roll(before, 7, 1), pltpu.roll(after, 1, 1))


def bands(low, high):
    shape = (LANES, LANES)
    i, j = sublanes_of(shape), lanes_of(shape)
    gap = jnp.abs(i - j)
    inside = (i >= low) & (i < high) & (j >= low) & (j < high)
    once = jnp.where(inside & (gap == 1), 1.0, 0.0)
    ends = jnp.where(i == low, 1.0, 0.0) + jnp.where(i == high - 1, 1.0, 0.0)
    twice = jnp.where(gap == 0, 2.0 - ends, jnp.where(gap == 2, 1.0, 0.0))
    return once, jnp.where(inside, twice, 0.0)


def half_form(field):
    zero = jnp.zeros_like(field[:1])
    return field * (jnp.concatenate([zero, field[:-1]], axis=0) + pltpu.roll(field, 1, 2))


GAMMA = (5.0 - 5.0**0.5) / 4.0
DELTA = (5.0 + 5.0**0.5) / 10.0


def moment_kernel(columns, place, held, extra, sums, kept, given, sigma):
    frames, channels = held.shape[:2]
    width = columns // BLOCKS
    halo = (LANES - width) // 2
    odd = place[2] > 0.5
    lane, sublane = lanes_of(TILE), sublanes_of(TILE)
    own = (lane >= halo) & (lane < halo + width)
    upper = (sublane % 2 == 0)[None]
    top = jnp.where(upper, place[0][None], 2.0)
    bottom = jnp.where(upper, 2.0, place[1][None])
    side = jnp.max(place[2])
    first_lane = jnp.where(side > 0.5, 0, halo)
    last_lane = jnp.where(side > 0.5, halo + width, LANES)
    matrix = jnp.concatenate([*bands(0, LANES), *bands(first_lane, last_lane)], axis=1)
    matrix = matrix.astype(jnp.bfloat16)
    rows = sublanes_of((2 * TILE[0], LANES)) % TILE[0] // 2
    edge = (rows == jnp.where(side > 0.5, BLOCKS // 2 - 1, 0))[None]
    result = jnp.zeros(TILE, jnp.float32)
    turn = first_member(frames) + 1
    for c in range(channels):
        b, g, h = [], [], []
        for p in range(2):
            both = jnp.concatenate([held[turn:, c, p], held[:turn, c, p]], axis=0)
            columned = jnp.dot(
                both.reshape(frames * 2 * TILE[0], LANES),
                matrix,
                preferred_element_type=jnp.float32,
            ).reshape(frames, 2 * TILE[0], 4 * LANES)
            plain, twice, cut, cut_twice = (
                columned[:, :, k * LANES : (k + 1) * LANES] for k in range(4)
            )
            for into, values in (
                (b, both.astype(jnp.float32)),
                (g, jnp.where(edge, cut, plain)),
                (h, jnp.where(edge, cut_twice, twice)),
            ):
                into += [values[:, : TILE[0]], values[:, TILE[0] :]]
        b_sums = [b[i] + b[i + 1] for i in range(3)]
        g_sums = [g[i] + g[i + 1] for i in range(3)]
        totals = [jnp.zeros(TILE, jnp.float32) for _ in range(6)]
        totals[5] = extra[c]
        sides = []
        for i in (1, 2):
            u0 = b[i]
            u1 = rows_of(b_sums[i - 1], b_sums[i])
            u2 = b[i - 1] + (top if i == 1 else bottom) * u0 + b[i + 1]
            k0 = frames_of(u0) + g[i]
            k1 = frames_of(u1) + rows_of(g_sums[i - 1], g_sums[i])
            kk0 = frames_of(k0 + g[i]) + h[i]
            n1 = u1 + k0
            n2 = u2 + 2.0 * k1 + kk0
            z = kk0 + 2.5 * k1 + GAMMA * u2
            t = u2 + DELTA * k1
            sides.append((u0, n1, n2))
            products = [
                u0 * u0,
                u0 * n1,
                n1 * n1,
                n1 * n2,
                n2 * n2,
                2.0 * half_form(z) + (2.0 * (5.0 - GAMMA * GAMMA)) * half_form(t),
            ]
            for k, product in enumerate(products):
                totals[k] = totals[k] + jnp.sum(product, axis=0)
        for k in range(3):
            kept[k, c] = jnp.where(odd[None], sides[1][k], sides[0][k])
            given[k, c] = jnp.where(odd[None], sides[0][k], sides[1][k])
        lines = jnp.zeros(TILE, jnp.float32)
        for k, total in enumerate(totals):
            total = jnp.sum(jnp.where(own, total, 0.0), axis=0, keepdims=True)
            lines = jnp.where(sublane == k, total, lines)
        column = jnp.sum(lines, axis=1, keepdims=True)
        result = jnp.where(lane == 8 * sublane + c, column, result)
    result = jnp.sum(result, axis=0, keepdims=True)
    sums[...] = jnp.broadcast_to(result[None], sums.shape)
    sigma[...] = extra[channels]


def combine_kernel(columns, place, sigma_at, sums, kept, taken, out):
    channels, frames = kept.shape[1:3]
    width = columns // BLOCKS
    halo = (LANES - width) // 2
    lane = lanes_of((1, LANES))
    total = jnp.sum(sums[...], axis=0)
    nu = [total] + [pltpu.roll(total, LANES - 8 * k, 1) for k in range(1, 6)]
    sigma = sigma_at[:1]
    g = [sigma * nu[k] - nu[k + 1] for k in range(5)]
    l1 = g[1] / g[0]
    l2 = g[2] / g[0]
    d1 = g[2] - l1 * g[1]
    e = g[3] - l1 * g[2]
    m = e / d1
    d2 = g[4] - l2 * g[2] - m * e
    z0 = nu[0]
    z1 = nu[1] - l1 * z0
    z2 = nu[2] - l2 * z0 - m * z1
    c2 = z2 / d2
    c1 = z1 / d1 - m * c2
    c0 = z0 / g[0] - l1 * c1 - l2 * c2

    tile_lane = lanes_of(TILE)
    tiles = -(-columns // LANES)
    odd = place[2] > 0.5
    for c in range(channels):
        w = [jnp.sum(jnp.where(lane == c, w, 0.0), axis=1, keepdims=True) for w in (c0, c1, c2)]
        for f in range(0, frames, 4):
            mine, other = [], []
            for i in range(f, f + 4):
                x = w[0] * kept[0, c, i] + w[1] * kept[1, c, i] + w[2] * kept[2, c, i]
                z = w[0] * taken[0, c, i] + w[1] * taken[1, c, i] + w[2] * taken[2, c, i]
                mine.append(jnp.where(odd, z, x))
                other.append(jnp.where(odd, x, z))
            turned = turn_pairs(mine) + turn_pairs(other)
            moved = [pltpu.roll(turned[s], (s * width - halo) % LANES, 1) for s in range(BLOCKS)]
            for t in range(tiles):
                piece = moved[t]
                if t + 1 < BLOCKS:
                    bound = width * (t + 1) - LANES * t
                    piece = jnp.where(tile_lane < bound, moved[t], moved[t + 1])
                count = min(LANES, columns - LANES * t)
                for i in range(4):
                    out[frames - 1 - (f + i), c, :, LANES * t : LANES * t + count] = piece[
                        2 * i : 2 * i + 2, :count
                    ]


def vmem():
    return pl.BlockSpec(memory_space=pltpu.VMEM)


def hbm():
    return pl.BlockSpec(memory_space=pltpu.HBM)


def params():
    return pltpu.CompilerParams(vmem_limit_bytes=32 << 20)


def shards(video, w_in, b_in, w_out, b_out, screen):
    count, me = lax.axis_size(AXIS), lax.axis_index(AXIS)
    _, channels, rows, columns = video.shape
    units = b_in.shape[0]
    frames = count
    operands = (w_in.T, b_in, w_out, b_out, screen, video)
    chunk = (channels, 2, 16, LANES)
    chunks = pl.pallas_call(
        grade_kernel,
        out_shape=jax.ShapeDtypeStruct((count,) + chunk, jnp.bfloat16),
        in_specs=[hbm()] * 6,
        out_specs=hbm(),
        scratch_shapes=[pltpu.SMEM(a.shape, a.dtype) for a in operands[:-1]]
        + [
            pltpu.VMEM(video.shape, video.dtype),
            pltpu.SemaphoreType.DMA((5 + rows // 16,)),
            pltpu.SemaphoreType.DMA((channels,)),
            pltpu.VMEM((channels, 2, rows // 2) + TILE, jnp.float32),
            pltpu.VMEM((8 * units, LANES), jnp.float32),
            pltpu.VMEM((channels, units) + TILE, jnp.float32),
            pltpu.VMEM((channels, count) + chunk[1:], jnp.bfloat16),
        ],
        name="grade",
    )(*operands)
    extra = pl.pallas_call(
        fifth_kernel,
        out_shape=jax.ShapeDtypeStruct((channels + 1,) + TILE, jnp.float32),
        in_specs=[pl.BlockSpec(memory_space=pltpu.SMEM), vmem()],
        out_specs=vmem(),
        compiler_params=params(),
        cost_estimate=pl.CostEstimate(flops=1 << 20, bytes_accessed=1 << 20, transcendentals=0),
        name="fifth",
    )(screen, chunks)
    first = first_member(count)
    order = [(first - i) % count for i in range(count)]
    held = lax.all_to_all(chunks, AXIS, 0, 0, axis_index_groups=[order])
    ends = [jnp.where(me // 2 == e, 1.0, 2.0) for e in (0, count // 2 - 1)]
    place = jnp.stack(ends + [jnp.where(me % 2 == 1, 1.0, 0.0)])
    place = jnp.broadcast_to(place[:, None, None], (3,) + TILE)
    fields = jax.ShapeDtypeStruct((3, channels, frames) + TILE, jnp.float32)
    sums, kept, given, sigma = pl.pallas_call(
        functools.partial(moment_kernel, columns),
        out_shape=(
            jax.ShapeDtypeStruct((count, 1, LANES), jnp.float32),
            fields,
            fields,
            jax.ShapeDtypeStruct(TILE, jnp.float32),
        ),
        in_specs=[vmem()] * 3,
        out_specs=(vmem(),) * 4,
        compiler_params=params(),
        name="moments",
    )(place, held, extra)
    taken = lax.ppermute(given, AXIS, [(i, i ^ 1) for i in range(count)])
    down = list(range(count))[::-1]
    sums = lax.all_to_all(sums, AXIS, 0, 0, axis_index_groups=[down])
    return pl.pallas_call(
        functools.partial(combine_kernel, columns),
        out_shape=jax.ShapeDtypeStruct((frames, channels, 2, columns), jnp.float32),
        in_specs=[vmem()] * 5,
        out_specs=vmem(),
        compiler_params=params(),
        name="combine",
    )(place, sigma, sums, kept, taken)


def solution(mesh):
    in_specs = (P(("video", AXIS), None, None, None), P(), P(), P(), P(), P())
    out_specs = P("video", None, AXIS, None)
    return jax.shard_map(shards, mesh=mesh, in_specs=in_specs, out_specs=out_specs, check_vma=False)
```

```python
import functools

import jax
import jax.numpy as jnp
from jax import lax
from jax.experimental import pallas as pl
from jax.experimental.pallas import tpu as pltpu
from jax.sharding import PartitionSpec as P

BLOCKS = 8
LANES = 128
TILE = (8, LANES)
AXIS = "tm"


def lanes_of(shape):
    return lax.broadcasted_iota(jnp.int32, shape, len(shape) - 1)


def sublanes_of(shape):
    return lax.broadcasted_iota(jnp.int32, shape, len(shape) - 2)


def first_member(count):
    return max(count * 3 // 4 - 1, 0)


def turn_pairs(tiles):
    sublane = sublanes_of(TILE)
    lower, even = sublane < 4, sublane % 4 < 2
    mixed = []
    for i in (0, 1):
        a, b = tiles[i], tiles[i + 2]
        mixed.append(
            (jnp.where(lower, a, pltpu.roll(b, 4, 0)), jnp.where(lower, pltpu.roll(a, 4, 0), b))
        )
    turned = []
    for i in (0, 1):
        a, b = mixed[0][i], mixed[1][i]
        turned.append(jnp.where(even, a, pltpu.roll(b, 2, 0)))
        turned.append(jnp.where(even, pltpu.roll(a, 6, 0), b))
    return turned


def three_parts(values, lane):
    high = values.astype(jnp.bfloat16).astype(jnp.float32)
    rest = values - high
    middle = rest.astype(jnp.bfloat16).astype(jnp.float32)
    third = LANES // 4
    return jnp.where(lane < third, high, jnp.where(lane < 2 * third, middle, rest - middle))


def grade_kernel(
    w_in_at, b_in_at, w_out_at, b_out_at, screen_at, video_at, chunks,
    w_in, b_in, w_out, b_out, screen, video, arrived, sent, graded, first, ready,
):
    channels, rows, columns = video.shape[1:]
    units = b_in.shape[0]
    across = -(-columns // LANES) * LANES
    width = columns // BLOCKS
    halo = (LANES - width) // 2
    chips = chunks.shape[0] // 2
    weights = [
        pltpu.make_async_copy(source, to, arrived.at[i])
        for i, (source, to) in enumerate(
            [
                (w_in_at, w_in), (b_in_at, b_in), (w_out_at, w_out),
                (b_out_at, b_out), (screen_at, screen),
            ]
        )
    ]

    def pixels_in(step):
        part = (slice(None), slice(None), pl.ds(pl.multiple_of(step * 16, 16), 16))
        return pltpu.make_async_copy(video_at.at[part], video.at[part], arrived.at[5 + step])

    for step in range(rows // 16):
        pixels_in(step).start()
    for copy in weights:
        copy.start()
    for copy in weights:
        copy.wait()

    lane, sublane = lanes_of(TILE), sublanes_of(TILE)
    part = lane % (LANES // 4)
    used = lane < 3 * (LANES // 4)
    picks = [jnp.where(used & (part == 8 * c + sublane), 0.5, 0.0) for c in range(channels)]
    ones = jnp.where(used & (part == 8 * channels), 0.5, 0.0)
    mix = [[jnp.zeros(TILE, jnp.float32) for _ in range(channels + 1)] for _ in range(channels)]
    for j in range(units):
        into = [jnp.full(TILE, w_in[c, j]) for c in range(channels)] + [jnp.full(TILE, b_in[j])]
        values = ones * into[channels]
        for c in range(channels):
            values = values + picks[c] * into[c]
        first[8 * j : 8 * j + 8] = three_parts(values, lane)
        for c in range(channels):
            out = jnp.full(TILE, w_out[c, j])
            for k in range(channels + 1):
                mix[c][k] = mix[c][k] + (0.5 * out) * into[k]
    for c in range(channels):
        mix[c][c] = mix[c][c] + 1.0
        mix[c][channels] = mix[c][channels] + b_out[c]
    layer = first[...].astype(jnp.bfloat16)

    half_blocks = BLOCKS // 2
    span = half_blocks * LANES
    zero = jnp.zeros(TILE, jnp.float32)
    upper = sublane % 2 == 0
    masks = []
    for side in range(2):
        column = (sublane // 2 + side * half_blocks) * width - halo + lane
        masks.append((column >= 0) & (column < columns))

    def wide(tile):
        return jnp.tile(tile, (1, half_blocks))

    def cut(band):
        parts = []
        for s in range(BLOCKS):
            start = s * width - halo
            v, off = start // LANES, start % LANES
            low = band[:, v * LANES : (v + 1) * LANES] if v >= 0 else zero
            high = band[:, (v + 1) * LANES : (v + 2) * LANES]
            parts.append(pltpu.roll(jnp.where(lane >= off, low, high), LANES - off, 1))
        return turn_pairs(parts[:half_blocks]), turn_pairs(parts[half_blocks:])

    def grade(step, _):
        pixels_in(step).wait()
        top = pl.multiple_of(step * 16, 16)
        taken = []
        for c in range(channels):
            values = video[0, c, pl.ds(top, 16), :].astype(jnp.float32)
            empty = jnp.zeros((16, across - columns), jnp.float32)
            taken.append(jnp.concatenate([values, empty], axis=1))
        for r in (0, 8):
            sides = [cut(values[r : r + 8]) for values in taken]
            for side in range(2):
                pixels = [jnp.concatenate(sides[c][side], axis=1) for c in range(channels)]
                group = jnp.concatenate(pixels + [jnp.ones((8, span), jnp.float32)], axis=0)
                group = group.astype(jnp.bfloat16)
                group = jnp.concatenate([group] * 3 + [jnp.zeros_like(group)], axis=0)
                half = jnp.dot(layer, group, preferred_element_type=jnp.float32)
                total = []
                for c in range(channels):
                    linear = wide(mix[c][channels])
                    for k in range(channels):
                        linear = linear + wide(mix[c][k]) * pixels[k]
                    total.append(linear)
                for j in range(units):
                    h = half[8 * j : 8 * j + 8]
                    unit = h * jnp.tanh(h)
                    for c in range(channels):
                        total[c] = total[c] + w_out[c, j] * unit
                for c in range(channels):
                    for k in range(half_blocks):
                        tile = total[c][:, k * LANES : (k + 1) * LANES]
                        at = step * 8 + r // 2 + k
                        graded[c, side, at] = jnp.where(masks[side], tile, 0.0)
        return 0

    lax.fori_loop(0, rows // 16, grade, 0, unroll=2)

    pairs = rows // 2
    copies = []
    for c in range(channels):
        for side in range(2):
            field = [graded[c, side, k] for k in range(pairs)]
            between = [
                field[0], *[field[k] + field[k + 1] for k in range(pairs - 1)], field[pairs - 1]
            ]
            target = [zero]
            for k in range(pairs):
                beyond = jnp.where(
                    upper, pltpu.roll(between[k], 7, 0), pltpu.roll(between[k + 1], 1, 0)
                )
                beyond = beyond + (pltpu.roll(field[k], 1, 1) + pltpu.roll(field[k], LANES - 1, 1))
                value = (screen[c] + 4.0) * field[k] - beyond
                target.append(jnp.where(masks[side], value, 0.0))
            target.append(zero)
            for q in range(chips):
                at = (first_member(2 * chips) - (2 * q + side)) % (2 * chips)
                for p in range(2):
                    k = 2 * q + 2 * p
                    both = jnp.concatenate([target[k], target[k + 1]], axis=0)
                    ready[c, at, p] = both.astype(jnp.bfloat16)
        copies.append(pltpu.make_async_copy(ready.at[c], chunks.at[:, c], sent.at[c]))
        copies[-1].start()
    for copy in copies:
        copy.wait()


def fifth_kernel(screen, chunks, extra):
    chips, channels = chunks.shape[0] // 2, chunks.shape[1]
    upper = sublanes_of(TILE) % 2 == 0
    zero = jnp.zeros(TILE, jnp.float32)
    sigma = jnp.full(TILE, 1.0, jnp.float32)
    pairs = 2 * chips
    for c in range(channels):
        sigma = jnp.where(lanes_of(TILE) == c, 6.0 + screen[c], sigma)
        total = zero
        for side in range(2):
            field = []
            for q in range(chips):
                at = (first_member(2 * chips) - (2 * q + side)) % (2 * chips)
                field.append(chunks[at, c, 0].astype(jnp.float32)[8:])
                field.append(chunks[at, c, 1].astype(jnp.float32)[:8])
            twice = []
            for k in range(pairs):
                beyond = zero
                if k > 0:
                    beyond = beyond + field[k - 1]
                if k < pairs - 1:
                    beyond = beyond + field[k + 1]
                own = 2.0 * field[k]
                if k == 0:
                    own = jnp.where(upper, field[k], own)
                if k == pairs - 1:
                    own = jnp.where(upper, own, field[k])
                twice.append(own + beyond)
            for k in range(pairs):
                after = pltpu.roll(twice[k + 1], 1, 0) if k < pairs - 1 else zero
                total = total + twice[k] * jnp.where(upper, pltpu.roll(twice[k], 7, 0), after)
        extra[c] = total + total
    extra[channels] = sigma


def frames_of(field):
    zero = jnp.zeros_like(field[:1])
    return jnp.concatenate([field[1:], zero], axis=0) + jnp.concatenate([zero, field[:-1]], axis=0)


def rows_of(before, after):
    upper = (sublanes_of(TILE) % 2 == 0)[None]
    return jnp.where(upper, pltpu.roll(before, 7, 1), pltpu.roll(after, 1, 1))


def bands(low, high):
    shape = (LANES, LANES)
    i, j = sublanes_of(shape), lanes_of(shape)
    gap = jnp.abs(i - j)
    inside = (i >= low) & (i < high) & (j >= low) & (j < high)
    once = jnp.where(inside & (gap == 1), 1.0, 0.0)
    ends = jnp.where(i == low, 1.0, 0.0) + jnp.where(i == high - 1, 1.0, 0.0)
    twice = jnp.where(gap == 0, 2.0 - ends, jnp.where(gap == 2, 1.0, 0.0))
    return once, jnp.where(inside, twice, 0.0)


def half_form(field):
    zero = jnp.zeros_like(field[:1])
    return field * (jnp.concatenate([zero, field[:-1]], axis=0) + pltpu.roll(field, 1, 2))


GAMMA = (5.0 - 5.0**0.5) / 4.0
DELTA = (5.0 + 5.0**0.5) / 10.0


def moment_kernel(columns, place, held, extra, sums, kept, given, sigma):
    frames, channels = held.shape[:2]
    width = columns // BLOCKS
    halo = (LANES - width) // 2
    odd = place[2] > 0.5
    lane, sublane = lanes_of(TILE), sublanes_of(TILE)
    own = (lane >= halo) & (lane < halo + width)
    upper = (sublane % 2 == 0)[None]
    top = jnp.where(upper, place[0][None], 2.0)
    bottom = jnp.where(upper, 2.0, place[1][None])
    side = jnp.max(place[2])
    first_lane = jnp.where(side > 0.5, 0, halo)
    last_lane = jnp.where(side > 0.5, halo + width, LANES)
    matrix = jnp.concatenate([*bands(0, LANES), *bands(first_lane, last_lane)], axis=1)
    matrix = matrix.astype(jnp.bfloat16)
    rows = sublanes_of((2 * TILE[0], LANES)) % TILE[0] // 2
    edge = (rows == jnp.where(side > 0.5, BLOCKS // 2 - 1, 0))[None]
    result = jnp.zeros(TILE, jnp.float32)
    turn = first_member(frames) + 1
    for c in range(channels):
        b, g, h = [], [], []
        for p in range(2):
            both = jnp.concatenate([held[turn:, c, p], held[:turn, c, p]], axis=0)
            columned = jnp.dot(
                both.reshape(frames * 2 * TILE[0], LANES),
                matrix,
                preferred_element_type=jnp.float32,
            ).reshape(frames, 2 * TILE[0], 4 * LANES)
            plain, twice, cut, cut_twice = (
                columned[:, :, k * LANES : (k + 1) * LANES] for k in range(4)
            )
            for into, values in (
                (b, both.astype(jnp.float32)),
                (g, jnp.where(edge, cut, plain)),
                (h, jnp.where(edge, cut_twice, twice)),
            ):
                into += [values[:, : TILE[0]], values[:, TILE[0] :]]
        b_sums = [b[i] + b[i + 1] for i in range(3)]
        g_sums = [g[i] + g[i + 1] for i in range(3)]
        totals = [jnp.zeros(TILE, jnp.float32) for _ in range(6)]
        totals[5] = extra[c]
        sides = []
        for i in (1, 2):
            u0 = b[i]
            u1 = rows_of(b_sums[i - 1], b_sums[i])
            u2 = b[i - 1] + (top if i == 1 else bottom) * u0 + b[i + 1]
            k0 = frames_of(u0) + g[i]
            k1 = frames_of(u1) + rows_of(g_sums[i - 1], g_sums[i])
            kk0 = frames_of(k0 + g[i]) + h[i]
            n1 = u1 + k0
            n2 = u2 + 2.0 * k1 + kk0
            z = kk0 + 2.5 * k1 + GAMMA * u2
            t = u2 + DELTA * k1
            sides.append((u0, n1, n2))
            products = [
                u0 * u0,
                u0 * n1,
                n1 * n1,
                n1 * n2,
                n2 * n2,
                2.0 * half_form(z) + (2.0 * (5.0 - GAMMA * GAMMA)) * half_form(t),
            ]
            for k, product in enumerate(products):
                totals[k] = totals[k] + jnp.sum(product, axis=0)
        for k in range(3):
            kept[k, c] = jnp.where(odd[None], sides[1][k], sides[0][k])
            given[k, c] = jnp.where(odd[None], sides[0][k], sides[1][k])
        lines = jnp.zeros(TILE, jnp.float32)
        for k, total in enumerate(totals):
            total = jnp.sum(jnp.where(own, total, 0.0), axis=0, keepdims=True)
            lines = jnp.where(sublane == k, total, lines)
        column = jnp.sum(lines, axis=1, keepdims=True)
        result = jnp.where(lane == 8 * sublane + c, column, result)
    result = jnp.sum(result, axis=0, keepdims=True)
    sums[...] = jnp.broadcast_to(result[None], sums.shape)
    sigma[...] = extra[channels]


def combine_kernel(columns, place, sigma_at, sums, kept, taken, out):
    channels, frames = kept.shape[1:3]
    width = columns // BLOCKS
    halo = (LANES - width) // 2
    lane = lanes_of((1, LANES))
    total = jnp.sum(sums[...], axis=0)
    nu = [total] + [pltpu.roll(total, LANES - 8 * k, 1) for k in range(1, 6)]
    sigma = sigma_at[:1]
    g = [sigma * nu[k] - nu[k + 1] for k in range(5)]
    l1 = g[1] / g[0]
    l2 = g[2] / g[0]
    d1 = g[2] - l1 * g[1]
    e = g[3] - l1 * g[2]
    m = e / d1
    d2 = g[4] - l2 * g[2] - m * e
    z0 = nu[0]
    z1 = nu[1] - l1 * z0
    z2 = nu[2] - l2 * z0 - m * z1
    c2 = z2 / d2
    c1 = z1 / d1 - m * c2
    c0 = z0 / g[0] - l1 * c1 - l2 * c2

    tile_lane = lanes_of(TILE)
    tiles = -(-columns // LANES)
    odd = place[2] > 0.5
    for c in range(channels):
        w = [jnp.sum(jnp.where(lane == c, w, 0.0), axis=1, keepdims=True) for w in (c0, c1, c2)]
        for f in range(0, frames, 4):
            mine, other = [], []
            for i in range(f, f + 4):
                x = w[0] * kept[0, c, i] + w[1] * kept[1, c, i] + w[2] * kept[2, c, i]
                z = w[0] * taken[0, c, i] + w[1] * taken[1, c, i] + w[2] * taken[2, c, i]
                mine.append(jnp.where(odd, z, x))
                other.append(jnp.where(odd, x, z))
            turned = turn_pairs(mine) + turn_pairs(other)
            moved = [pltpu.roll(turned[s], (s * width - halo) % LANES, 1) for s in range(BLOCKS)]
            for t in range(tiles):
                piece = moved[t]
                if t + 1 < BLOCKS:
                    bound = width * (t + 1) - LANES * t
                    piece = jnp.where(tile_lane < bound, moved[t], moved[t + 1])
                count = min(LANES, columns - LANES * t)
                for i in range(4):
                    out[frames - 1 - (f + i), c, :, LANES * t : LANES * t + count] = piece[
                        2 * i : 2 * i + 2, :count
                    ]


def vmem():
    return pl.BlockSpec(memory_space=pltpu.VMEM)


def hbm():
    return pl.BlockSpec(memory_space=pltpu.HBM)


def params():
    return pltpu.CompilerParams(vmem_limit_bytes=32 << 20)


def shards(video, w_in, b_in, w_out, b_out, screen):
    count, me = lax.axis_size(AXIS), lax.axis_index(AXIS)
    _, channels, rows, columns = video.shape
    units = b_in.shape[0]
    frames = count
    operands = (w_in.T, b_in, w_out, b_out, screen, video)
    chunk = (channels, 2, 16, LANES)
    chunks = pl.pallas_call(
        grade_kernel,
        out_shape=jax.ShapeDtypeStruct((count,) + chunk, jnp.bfloat16),
        in_specs=[hbm()] * 6,
        out_specs=hbm(),
        scratch_shapes=[pltpu.SMEM(a.shape, a.dtype) for a in operands[:-1]]
        + [
            pltpu.VMEM(video.shape, video.dtype),
            pltpu.SemaphoreType.DMA((5 + rows // 16,)),
            pltpu.SemaphoreType.DMA((channels,)),
            pltpu.VMEM((channels, 2, rows // 2) + TILE, jnp.float32),
            pltpu.VMEM((8 * units, LANES), jnp.float32),
            pltpu.VMEM((channels, count) + chunk[1:], jnp.bfloat16),
        ],
        name="grade",
    )(*operands)
    extra = pl.pallas_call(
        fifth_kernel,
        out_shape=jax.ShapeDtypeStruct((channels + 1,) + TILE, jnp.float32),
        in_specs=[pl.BlockSpec(memory_space=pltpu.SMEM), vmem()],
        out_specs=vmem(),
        compiler_params=params(),
        cost_estimate=pl.CostEstimate(flops=1 << 20, bytes_accessed=1 << 20, transcendentals=0),
        name="fifth",
    )(screen, chunks)
    first = first_member(count)
    order = [(first - i) % count for i in range(count)]
    held = lax.all_to_all(chunks, AXIS, 0, 0, axis_index_groups=[order])
    ends = [jnp.where(me // 2 == e, 1.0, 2.0) for e in (0, count // 2 - 1)]
    place = jnp.stack(ends + [jnp.where(me % 2 == 1, 1.0, 0.0)])
    place = jnp.broadcast_to(place[:, None, None], (3,) + TILE)
    fields = jax.ShapeDtypeStruct((3, channels, frames) + TILE, jnp.float32)
    sums, kept, given, sigma = pl.pallas_call(
        functools.partial(moment_kernel, columns),
        out_shape=(
            jax.ShapeDtypeStruct((count, 1, LANES), jnp.float32),
            fields,
            fields,
            jax.ShapeDtypeStruct(TILE, jnp.float32),
        ),
        in_specs=[vmem()] * 3,
        out_specs=(vmem(),) * 4,
        compiler_params=params(),
        name="moments",
    )(place, held, extra)
    taken = lax.ppermute(given, AXIS, [(i, i ^ 1) for i in range(count)])
    down = list(range(count))[::-1]
    sums = lax.all_to_all(sums, AXIS, 0, 0, axis_index_groups=[down])
    return pl.pallas_call(
        functools.partial(combine_kernel, columns),
        out_shape=jax.ShapeDtypeStruct((frames, channels, 2, columns), jnp.float32),
        in_specs=[vmem()] * 5,
        out_specs=vmem(),
        compiler_params=params(),
        name="combine",
    )(place, sigma, sums, kept, taken)


def solution(mesh):
    in_specs = (P(("video", AXIS), None, None, None), P(), P(), P(), P(), P())
    out_specs = P("video", None, AXIS, None)
    return jax.shard_map(shards, mesh=mesh, in_specs=in_specs, out_specs=out_specs, check_vma=False)
```
